128 devices in a mesh: req: 4 (over x), tile: 32 (over z, y, core).
Axes of the slice: x: 4, y: 4, z: 4, core: 2. Of those that a mesh axis runs over, the one named last changes fastest.
Arguments:
- latents: bfloat16 [8, 128, 80, 512], P('req', 'tile'), may hold values from -6 to 6
- lengths: int32 [4], replicated, may hold values from 1 to 4, 8 in all
- conv_first: bfloat16 [3, 3, 3, 512, 512], replicated, may hold values from -0.0546875 to 0.0546875
- conv_second: bfloat16 [3, 3, 3, 512, 512], replicated, may hold values from -0.0546875 to 0.0546875
- gain_first: float32 [512], replicated, may hold values from 0.1 to 1.9
- gain_second: float32 [512], replicated, may hold values from 0.1 to 1.9
Outputs:
- block_out: bfloat16 [8, 128, 80, 512], P('req', 'tile')
The draws below stay inside these ranges and needn't reach their ends.
Inputs may be any that keep to these rules, and one draw needn't show every extreme that they name: The lengths sum to 8; the longest clip has exactly 4 frames.
All inputs are finite; a program needn't handle non-finite values.
Results may differ from the reference program's by a relative error of at most 0.0038.
Values may be sent and summed in bfloat16 or wider, within the bound.
A program may use at most 128 MiB of HBM per device.

```python
import math
import jax
import jax.numpy as jnp
import numpy as np
from jax import lax

C = 512
GROUPS = 32
W = 80
CLIPS = 4
H = 128
SLOTS = 8
FRAMES = 4


def shard_levels(rng, dims, split, least, high):
    loudness, own = 1.0, jax.random.fold_in(rng, 6)
    for position, shards_of in split:
        draws = jnp.exp(jax.random.uniform(jax.random.fold_in(own, position), (shards_of,), jnp.float32, least / len(split), high / len(split)))
        loudness = loudness * jnp.repeat(draws, dims[position] // shards_of).reshape([-1 if axis == position else 1 for axis in range(len(dims))])
    return loudness


def length_profile(amount, total, bound, skew):
    loads = [(1 << 20) // math.isqrt(grade ** skew) + 1 for grade in range(2, amount + 1)]
    surplus, given = total - bound - (amount - 1), [1] * (amount - 1)
    while surplus > 0:
        movable = [i for i in range(amount - 1) if given[i] < bound]
        mass, left = sum([loads[i] for i in movable]), surplus
        for i in movable:
            addition = min(bound - given[i], max(1, left * loads[i] // mass), surplus)
            given[i] = given[i] + addition
            surplus = surplus - addition
    return np.array([bound] + given)


def ragged_sizes(stream_key, amount, total, bound, lean):
    if amount == 2:
        one = jax.random.randint(stream_key, (), max(1, total - bound), min(bound, total - 1) + 1)
        return jnp.stack([one, total - one])
    sizes = jnp.asarray(length_profile(amount, total, bound, lean), jnp.int32)
    twos = (amount - 1) // 2
    source_of, receiver = sizes[1:1 + 2 * twos:2], sizes[2:2 + 2 * twos:2]
    room = jnp.minimum(source_of - 1, bound - receiver)
    passed = jax.random.randint(jax.random.fold_in(stream_key, 1), (twos,), 0, 1 << 20) % (room + 1)
    sizes = sizes.at[1:1 + 2 * twos:2].set(source_of - passed).at[2:2 + 2 * twos:2].set(receiver + passed)
    return sizes[jax.random.permutation(jax.random.fold_in(stream_key, 2), amount)]


def centred(key, dims, scale, reach, cuts=(), kind=jnp.bfloat16):
    loudness = shard_levels(key, dims, cuts, -0.22, 0.18) if cuts else 1.0
    result = jax.random.normal(key, dims, jnp.float32) * scale * loudness
    return jnp.minimum(jnp.maximum(result, -reach), reach).astype(kind)


def setup_inputs(seed: int = 0) -> dict:
    splits = jax.random.split(jax.random.key(seed), 7)
    return {
        "latents": centred(splits[0], (SLOTS, H, W, C), 1.0, 6.0, ((0, 4), (1, 32))),
        "lengths": ragged_sizes(splits[1], CLIPS, SLOTS, FRAMES, 2).astype(jnp.int32),
        "conv_first": centred(splits[2], (3, 3, 3, C, C), (27 * C) ** -0.5, 0.0546875),
        "conv_second": centred(splits[3], (3, 3, 3, C, C), (27 * C) ** -0.5, 0.0546875),
        "gain_first": jnp.clip(1.0 + 0.18 * jax.random.normal(splits[4], (C,), jnp.float32), 0.1, 1.9),
        "gain_second": jnp.clip(1.0 + 0.18 * jax.random.normal(splits[5], (C,), jnp.float32), 0.1, 1.9),
    }


def clip_ids(slot_ids, lengths):
    starts = jnp.cumsum(lengths) - lengths
    return lax.optimization_barrier(jnp.sum((slot_ids[:, None] >= starts[None, :]).astype(jnp.int32), axis=1)) - 1

def group_stats(field, member, lengths, height, width):
    chans = field.shape[3]
    total = lax.optimization_barrier(jnp.sum(field.astype(jnp.float32), axis=(1, 2)))
    squares = lax.optimization_barrier(jnp.sum(jnp.square(field.astype(jnp.float32)), axis=(1, 2)))
    clip_total = jnp.dot(member.T, total, precision=lax.Precision.HIGHEST)
    clip_squares = jnp.dot(member.T, squares, precision=lax.Precision.HIGHEST)
    per_group = chans // GROUPS
    group_total = lax.optimization_barrier(jnp.sum(clip_total.reshape(-1, GROUPS, per_group), axis=2))
    group_squares = lax.optimization_barrier(jnp.sum(clip_squares.reshape(-1, GROUPS, per_group), axis=2))
    counts = lengths.astype(jnp.float32) * (height * width * per_group)
    mean = group_total / counts[:, None]
    rstd = lax.rsqrt(group_squares / counts[:, None] - mean * mean + 1e-06)
    mean_frame = jnp.dot(member, jnp.repeat(mean, per_group, axis=1), precision=lax.Precision.HIGHEST)
    rstd_frame = jnp.dot(member, jnp.repeat(rstd, per_group, axis=1), precision=lax.Precision.HIGHEST)
    return (mean_frame, rstd_frame)

def activate(field, mean_frame, rstd_frame, gain):
    scaled = (field.astype(jnp.float32) - mean_frame[:, None, None, :]) * rstd_frame[:, None, None, :] * gain
    return jax.nn.silu(scaled).astype(jnp.bfloat16)

def causal_conv(act, kernel, causal):
    slots, height, width, chans = act.shape
    padded = jnp.pad(act, ((2, 0), (1, 1), (1, 1), (0, 0)))
    taps = kernel.reshape(3, 9 * chans, chans).astype(jnp.float32)

    def frame_out(t):
        acc = jnp.zeros((height * width, chans), jnp.float32)
        for dt in range(3):
            frame = lax.dynamic_index_in_dim(padded, t + dt, 0, keepdims=False)
            pieces = [frame[dy:dy + height, dx:dx + width, :] for dy in range(3) for dx in range(3)]
            columns = jnp.concatenate(pieces, axis=-1).reshape(height * width, 9 * chans).astype(jnp.float32)
            acc = acc + causal[dt][t] * jnp.dot(columns, taps[dt], precision=lax.Precision.HIGHEST)
        return acc.reshape(height, width, chans)
    return lax.map(frame_out, jnp.arange(slots, dtype=jnp.int32))

def reference(latents, lengths, conv_first, conv_second, gain_first, gain_second):
    slots, height, width, chans = latents.shape
    slot_ids = jnp.arange(slots, dtype=jnp.int32)
    clip_here = clip_ids(slot_ids, lengths)
    clip_back = clip_ids(jnp.arange(slots + 2, dtype=jnp.int32) - 2, lengths)
    member = (clip_here[:, None] == jnp.arange(lengths.shape[0], dtype=jnp.int32)[None, :]).astype(jnp.float32)
    causal = [(clip_back[dt:dt + slots] == clip_here).astype(jnp.float32) for dt in range(3)]
    mean_one, rstd_one = group_stats(latents, member, lengths, height, width)
    act_first = activate(latents, mean_one, rstd_one, gain_first)
    mid = causal_conv(act_first, conv_first, causal)
    mean_two, rstd_two = group_stats(mid, member, lengths, height, width)
    act_second = activate(mid, mean_two, rstd_two, gain_second)
    final = causal_conv(act_second, conv_second, causal)
    return (latents.astype(jnp.float32) + final).astype(jnp.bfloat16)
```

```python
import functools

import jax
import jax.numpy as jnp
from jax import lax
from jax.experimental import pallas as pl
from jax.experimental.pallas import tpu as pltpu
from jax.sharding import PartitionSpec as P

GROUPS = 32
MESH = pl.DeviceIdType.MESH
F32 = jnp.float32
BF16 = jnp.bfloat16
NX, NY, NZ, NC = 4, 4, 4, 2
NT = NZ * NY * NC


def lane_ids(shape):
    return lax.broadcasted_iota(jnp.int32, shape, 1)


def swap_lanes(x, step):
    lanes = lane_ids(x.shape)
    return jnp.where((lanes & step) != 0, pltpu.roll(x, step, 1), pltpu.roll(x, 128 - step, 1))


def segment_sum(x):
    for step in (1, 2, 4, 8):
        x = x + swap_lanes(x, step)
    return x


def block_kernel(
    lengths, lat, w1_hbm, w2_hbm, gain1, gain2, out,
    w1, w2, x_raw, m_raw, act, acc, mid, stage, rows_scr, e_scr, p_scr, mean_scr, scale_scr,
    src1, buf1, src2, buf2, send_sem, recv_sem, local_sem,
):
    r = lax.axis_index("req")
    t = lax.axis_index("tile")
    cells = lat.shape[1] * lat.shape[2]
    width = lat.shape[2]
    z = t // (NY * NC)
    yc = lax.rem(t, NY * NC)
    right = (lax.rem(r + 1, NX), t)
    above = (r, lax.rem(t + NT - 1, NT))
    below = (r, lax.rem(t + 1, NT))
    peers1 = [(r, z * (NY * NC) + lax.rem(yc + j, NY * NC)) for j in range(1, NY * NC)]
    peers2 = [
        (lax.rem(r + j // NZ, NX), lax.rem(t + (NY * NC) * (j % NZ), NT)) for j in range(1, NX * NZ)
    ]

    barrier = pltpu.get_barrier_semaphore()
    greeted = peers1 + peers2 + [above, below]
    for peer in greeted:
        pl.semaphore_signal(barrier, inc=1, device_id=peer, device_id_type=MESH)

    lat_copy = pltpu.make_async_copy(lat, x_raw.at[2:4, 1:5], local_sem.at[0])
    lat_copy.start()
    w_copies = [
        pltpu.make_async_copy(w1_hbm, w1, local_sem.at[1]),
        pltpu.make_async_copy(w2_hbm, w2, local_sem.at[2]),
    ]
    for copy in w_copies:
        copy.start()

    used = [0]
    sent = []

    def send(src, dst, peer):
        i = used[0]
        used[0] += 1
        copy = pltpu.make_async_remote_copy(
            src_ref=src, dst_ref=dst, send_sem=send_sem.at[i], recv_sem=recv_sem.at[i],
            device_id=peer, device_id_type=MESH,
        )
        copy.start()
        sent.append(copy)
        return copy

    first = lengths[0]
    second = first + lengths[1]
    third = second + lengths[2]

    def one(condition):
        return jnp.where(condition, 1, 0)

    def clip(s):
        return one(s >= 0) + one(s >= first) + one(s >= second) + one(s >= third) - 1

    base = 2 * r
    clip_q = [clip(base - 2 + q) for q in range(4)]

    def same(a, b):
        return jnp.where(a == b, 1.0, 0.0).astype(F32)

    pair = {
        (0, 0): same(clip_q[0], clip_q[2]),
        (1, 0): same(clip_q[1], clip_q[2]),
        (0, 1): same(clip_q[1], clip_q[3]),
        (1, 1): same(clip_q[2], clip_q[3]),
    }

    def pack(use):
        sums = segment_sum(rows_scr[...])
        row = lax.broadcasted_iota(jnp.int32, (16, 128), 0)
        picked = jnp.where((lane_ids((16, 128)) & 15) == row, sums, 0.0)
        src1[use] = jnp.broadcast_to(jnp.sum(picked, axis=0, keepdims=True), (8, 128))

    def put_rows(frame, total, squares):
        for kind, value in enumerate((total, squares)):
            value = jnp.sum(value, axis=0, keepdims=True)
            for b in range(4):
                k = 4 * (2 * frame + kind) + b
                rows_scr[k : k + 1, :] = value[:, b * 128 : (b + 1) * 128]

    def exchange_one(use):
        return [send(src1.at[use], buf1.at[use, j], peer) for j, peer in enumerate(peers1)]

    def exchange_two(use, copies):
        for copy in copies:
            copy.wait_recv()
        total = src1[use]
        for j in range(len(peers1)):
            total = total + buf1[use, j]
        src2[use] = total
        return [send(src2.at[use], buf2.at[use, j], peer) for j, peer in enumerate(peers2)]

    def params(use, copies, gain):
        for copy in copies:
            copy.wait_recv()
        lanes = lane_ids((8, 128))
        parts = []
        for dx in range(NX):
            total = src2[use] if dx == 0 else buf2[use, NZ * dx - 1]
            for dz in range(1, NZ):
                total = total + buf2[use, NZ * dx + dz - 1]
            parts.append(total)
        row8 = lax.broadcasted_iota(jnp.int32, (8, 128), 0)
        early = (lanes & 8) == 0
        for q in range(4):
            mixed = jnp.zeros((8, 128), F32)
            count = jnp.float32(0.0)
            for dx in range(NX):
                rr = lax.rem(r + NX - dx, NX)
                m0 = same(clip(2 * rr), clip_q[q])
                m1 = same(clip(2 * rr + 1), clip_q[q])
                count = count + m0 + m1
                mixed = mixed + jnp.where(early, m0, m1) * parts[dx]
            mixed = mixed + swap_lanes(mixed, 8)
            e_scr[8 * q : 8 * q + 8] = jnp.where((lanes & 15) == row8, mixed, 0.0)
            p_scr[8 * q : 8 * q + 8] = jnp.full((8, 128), jnp.maximum(count, 1.0), F32)
        e_scr[...] = segment_sum(e_scr[...]) / (p_scr[...] * float(128 * 80 * 512 // GROUPS))
        for q in range(4):
            mean = e_scr[8 * q : 8 * q + 4]
            scale = lax.rsqrt(e_scr[8 * q + 4 : 8 * q + 8] - mean * mean + 1e-06) * gain[...]
            p_scr[4 * q : 4 * q + 4] = scale
        for q in range(4):
            for b in range(4):
                mean_scr[q : q + 1, b * 128 : (b + 1) * 128] = e_scr[8 * q + b : 8 * q + b + 1, :]
                scale_scr[q : q + 1, b * 128 : (b + 1) * 128] = p_scr[4 * q + b : 4 * q + b + 1, :]

    def activated(value, q):
        v = (value - mean_scr[q : q + 1, :]) * scale_scr[q : q + 1, :]
        half = 0.5 * v
        return half + half * jnp.tanh(half)

    def place(value, q, row):
        if q == 3:
            act[2, 1, row] = value.astype(BF16)
        elif q == 2:
            act[2, 0, row] = value.astype(BF16)
            act[1, 1, row] = (value * pair[1, 1]).astype(BF16)
        elif q == 1:
            act[1, 0, row] = (value * pair[1, 0]).astype(BF16)
            act[0, 1, row] = (value * pair[0, 1]).astype(BF16)
        else:
            act[0, 0, row] = (value * pair[0, 0]).astype(BF16)

    def inside(row):
        out_top = one(row == 0) * one(t == 0)
        out_bottom = one(row == 5) * one(t == NT - 1)
        return (1 - out_top - out_bottom).astype(F32)

    def activate_rows(raw, q):
        @pl.loop(0, 6)
        def _(row):
            place(activated(raw[q, row].astype(F32), q) * inside(row), q, row)

    def activate_wide(q):
        @pl.loop(0, 4)
        def _(row):
            place(activated(mid[q - 2, row], q), q, row + 1)

        for row in (0, 5):
            place(activated(m_raw[q, row].astype(F32), q) * inside(row), q, row)

    def conv_step(w, frame, dx):
        lhs = jnp.concatenate(
            [act[dt, frame, dy : dy + 4].reshape(cells, 512) for dt in range(3) for dy in range(3)],
            axis=-1,
        )
        for n in range(2):
            cols = slice(n * 256, (n + 1) * 256)
            rhs = jnp.concatenate(
                [w[dt, dy, dx, :, cols] for dt in range(3) for dy in range(3)], axis=0
            )
            acc[dx, :, cols] = jnp.dot(lhs, rhs, preferred_element_type=F32)

    def conv(w, frame, start, stop):
        @pl.loop(start, stop)
        def _(dx):
            conv_step(w, frame, dx)

    def conv_row(row):
        rows = pl.ds(pl.multiple_of(row * width, 16), width)
        column = lax.broadcasted_iota(jnp.int32, (width, 512), 0)
        low = jnp.where(column == 0, 0.0, pltpu.roll(acc[0, rows, :], 1, 0))
        high = jnp.where(column == width - 1, 0.0, pltpu.roll(acc[2, rows, :], width - 1, 0))
        return acc[1, rows, :] + low + high

    def sums_of(value):
        parts = value.reshape(width // 8, 8, 512)
        return jnp.sum(parts, axis=0), jnp.sum(parts * parts, axis=0)

    zero = jnp.zeros((8, 512), F32)

    lat_copy.wait()
    for frame in range(2):
        def latent_row(row, carry, frame=frame):
            total, squares = sums_of(x_raw[2 + frame, row + 1].astype(F32))
            return carry[0] + total, carry[1] + squares

        put_rows(frame, *lax.fori_loop(0, 4, latent_row, (zero, zero)))
    pack(0)
    pl.semaphore_wait(barrier, len(greeted))

    def send_frame(src_rows, dst, frame):
        edges = [send(src_rows(frame, row, 1), dst.at[frame, row + 1 : row + 2], right) for row in (0, 3)]
        inner = send(src_rows(frame, 1, 2), dst.at[frame, 2:4], right)
        return edges, inner

    def pass_edges(dst, q, edges):
        for edge in edges:
            edge.wait_recv()
        return [
            send(dst.at[q, 1:2], dst.at[q, 5:6], above),
            send(dst.at[q, 4:5], dst.at[q, 0:1], below),
        ]

    stats = exchange_one(0)

    def lat_rows(frame, row, n):
        return lat.at[frame, row : row + n]

    edges1, inner1 = send_frame(lat_rows, x_raw, 1)
    faces = [
        send(lat.at[0:2, 0:1], x_raw.at[2:4, 5:6], above),
        send(lat.at[0:2, 3:4], x_raw.at[2:4, 0:1], below),
    ]
    edges0, inner0 = send_frame(lat_rows, x_raw, 0)
    stats = exchange_two(0, stats)
    passed1 = pass_edges(x_raw, 1, edges1)
    params(0, stats, gain1)
    for copy in faces:
        copy.wait_recv()
    activate_rows(x_raw, 3)
    activate_rows(x_raw, 2)
    inner1.wait_recv()
    for copy in passed1:
        copy.wait_recv()
    activate_rows(x_raw, 1)
    w_copies[0].wait()
    conv(w1, 1, 0, 2)
    passed0 = pass_edges(x_raw, 0, edges0)
    conv(w1, 1, 2, 3)

    def finish_mid(frame):
        def mid_row(row, carry):
            value = conv_row(row)
            mid[frame, row] = value
            m_raw[2 + frame, row + 1] = value.astype(BF16)
            total, squares = sums_of(value)
            return carry[0] + total, carry[1] + squares

        put_rows(frame, *lax.fori_loop(0, 4, mid_row, (zero, zero)))

    def mid_rows(frame, row, n):
        return m_raw.at[2 + frame, row + 1 : row + 1 + n]

    def mid_faces(frame):
        return [
            send(m_raw.at[2 + frame, 1:2], m_raw.at[2 + frame, 5:6], above),
            send(m_raw.at[2 + frame, 4:5], m_raw.at[2 + frame, 0:1], below),
        ]

    finish_mid(1)
    edges1, inner1b = send_frame(mid_rows, m_raw, 1)
    faces = mid_faces(1)
    inner0.wait_recv()
    for copy in passed0:
        copy.wait_recv()
    activate_rows(x_raw, 0)
    conv(w1, 0, 0, 3)
    finish_mid(0)
    pack(1)
    stats = exchange_one(1)
    faces += mid_faces(0)
    edges0, inner0b = send_frame(mid_rows, m_raw, 0)
    passed1 = pass_edges(m_raw, 1, edges1)
    stats = exchange_two(1, stats)
    params(1, stats, gain2)
    for copy in faces:
        copy.wait_recv()
    activate_wide(3)
    activate_wide(2)
    inner1b.wait_recv()
    for copy in passed1:
        copy.wait_recv()
    activate_rows(m_raw, 1)
    w_copies[1].wait()
    passed0 = pass_edges(m_raw, 0, edges0)
    conv(w2, 1, 0, 3)

    def finish_out(frame):
        @pl.loop(0, 4)
        def _(row):
            stage[frame, row] = (x_raw[2 + frame, row + 1].astype(F32) + conv_row(row)).astype(BF16)

        copy = pltpu.make_async_copy(stage.at[frame], out.at[frame], local_sem.at[3 + frame])
        copy.start()
        return copy

    out1 = finish_out(1)
    inner0b.wait_recv()
    for copy in passed0:
        copy.wait_recv()
    activate_rows(m_raw, 0)
    conv(w2, 0, 0, 3)
    out0 = finish_out(0)
    for copy in sent:
        copy.wait_send()
    out1.wait()
    out0.wait()


N_SENDS = 2 * (NY * NC - 1) + 2 * (NX * NZ - 1) + 12 + 6 + 8


def shards(latents, lengths, conv_first, conv_second, gain_first, gain_second):
    frames, rows, width, chans = latents.shape
    smem = pl.BlockSpec(memory_space=pltpu.SMEM)
    vmem = pl.BlockSpec(memory_space=pltpu.VMEM)
    hbm = pl.BlockSpec(memory_space=pl.ANY)
    flops = 2 * 2 * frames * rows * width * 27 * chans * chans
    return pl.pallas_call(
        block_kernel,
        out_shape=jax.ShapeDtypeStruct(latents.shape, latents.dtype),
        in_specs=[smem, hbm, hbm, hbm, vmem, vmem],
        out_specs=hbm,
        scratch_shapes=[
            pltpu.VMEM(conv_first.shape, BF16),
            pltpu.VMEM(conv_second.shape, BF16),
            pltpu.VMEM((4, rows + 2, width, chans), BF16),
            pltpu.VMEM((4, rows + 2, width, chans), BF16),
            pltpu.VMEM((3, 2, rows + 2, width, chans), BF16),
            pltpu.VMEM((3, rows * width, chans), F32),
            pltpu.VMEM((2, rows, width, chans), F32),
            pltpu.VMEM((2, rows, width, chans), BF16),
            pltpu.VMEM((16, 128), F32),
            pltpu.VMEM((32, 128), F32),
            pltpu.VMEM((32, 128), F32),
            pltpu.VMEM((8, chans), F32),
            pltpu.VMEM((8, chans), F32),
            pltpu.VMEM((2, 8, 128), F32),
            pltpu.VMEM((2, NY * NC - 1, 8, 128), F32),
            pltpu.VMEM((2, 8, 128), F32),
            pltpu.VMEM((2, NX * NZ - 1, 8, 128), F32),
            pltpu.SemaphoreType.DMA((N_SENDS,)),
            pltpu.SemaphoreType.DMA((N_SENDS,)),
            pltpu.SemaphoreType.DMA((5,)),
        ],
        compiler_params=pltpu.CompilerParams(
            collective_id=0, has_side_effects=True, vmem_limit_bytes=60 * 2**20
        ),
        cost_estimate=pl.CostEstimate(
            flops=flops, bytes_accessed=2 * conv_first.size * 2 + 2 * latents.size * 2, transcendentals=latents.size * 6
        ),
    )(
        lengths, latents, conv_first, conv_second,
        gain_first.reshape(4, chans // 4), gain_second.reshape(4, chans // 4),
    )


def solution(mesh):
    return jax.shard_map(
        shards,
        mesh=mesh,
        in_specs=(P("req", "tile", None, None), P(), P(), P(), P(), P()),
        out_specs=P("req", "tile", None, None),
        check_vma=False,
    )
```

```python
import functools

import jax
import jax.numpy as jnp
from jax import lax
from jax.experimental import pallas as pl
from jax.experimental.pallas import tpu as pltpu
from jax.sharding import PartitionSpec as P

GROUPS = 32
MESH = pl.DeviceIdType.MESH
F32 = jnp.float32
BF16 = jnp.bfloat16
NX, NY, NZ, NC = 4, 4, 4, 2
NT = NZ * NY * NC


def lane_ids(shape):
    return lax.broadcasted_iota(jnp.int32, shape, 1)


def swap_lanes(x, step):
    lanes = lane_ids(x.shape)
    return jnp.where((lanes & step) != 0, pltpu.roll(x, step, 1), pltpu.roll(x, 128 - step, 1))


def segment_sum(x):
    for step in (1, 2, 4, 8):
        x = x + swap_lanes(x, step)
    return x


def block_kernel(
    lengths, lat, w1_hbm, w2_hbm, gain1, gain2, out,
    w1, w2, x_raw, m_raw, act, acc, mid, stage, rows_scr, e_scr, p_scr, mean_scr, scale_scr,
    src1, buf1, src2, buf2, send_sem, recv_sem, local_sem,
):
    r = lax.axis_index("req")
    t = lax.axis_index("tile")
    cells = lat.shape[1] * lat.shape[2]
    width = lat.shape[2]
    z = t // (NY * NC)
    yc = lax.rem(t, NY * NC)
    right = (lax.rem(r + 1, NX), t)
    above = (r, lax.rem(t + NT - 1, NT))
    below = (r, lax.rem(t + 1, NT))
    peers1 = [
        (lax.rem(r + j // NZ, NX), lax.rem(t + (NY * NC) * (j % NZ), NT)) for j in range(1, NX * NZ)
    ]
    peers2 = [(r, z * (NY * NC) + lax.rem(yc + j, NY * NC)) for j in range(1, NY * NC)]

    barrier = pltpu.get_barrier_semaphore()
    greeted = peers1 + peers2 + [above, below]
    for peer in greeted:
        pl.semaphore_signal(barrier, inc=1, device_id=peer, device_id_type=MESH)

    lat_copy = pltpu.make_async_copy(lat, x_raw.at[2:4, 1:5], local_sem.at[0])
    lat_copy.start()
    w_copies = [
        pltpu.make_async_copy(w1_hbm, w1, local_sem.at[1]),
        pltpu.make_async_copy(w2_hbm, w2, local_sem.at[2]),
    ]
    for copy in w_copies:
        copy.start()

    used = [0]
    sent = []

    def send(src, dst, peer):
        i = used[0]
        used[0] += 1
        copy = pltpu.make_async_remote_copy(
            src_ref=src, dst_ref=dst, send_sem=send_sem.at[i], recv_sem=recv_sem.at[i],
            device_id=peer, device_id_type=MESH,
        )
        copy.start()
        sent.append(copy)
        return copy

    first = lengths[0]
    second = first + lengths[1]
    third = second + lengths[2]

    def one(condition):
        return jnp.where(condition, 1, 0)

    def clip(s):
        return one(s >= 0) + one(s >= first) + one(s >= second) + one(s >= third) - 1

    base = 2 * r
    clip_q = [clip(base - 2 + q) for q in range(4)]

    def same(a, b):
        return jnp.where(a == b, 1.0, 0.0).astype(F32)

    pair = {
        (0, 0): same(clip_q[0], clip_q[2]),
        (1, 0): same(clip_q[1], clip_q[2]),
        (0, 1): same(clip_q[1], clip_q[3]),
        (1, 1): same(clip_q[2], clip_q[3]),
    }

    def pack(use):
        sums = segment_sum(rows_scr[...])
        row = lax.broadcasted_iota(jnp.int32, (16, 128), 0)
        picked = jnp.where((lane_ids((16, 128)) & 15) == row, sums, 0.0)
        src1[use] = jnp.broadcast_to(jnp.sum(picked, axis=0, keepdims=True), (8, 128))

    def put_rows(frame, total, squares):
        for kind, value in enumerate((total, squares)):
            value = jnp.sum(value, axis=0, keepdims=True)
            for b in range(4):
                k = 4 * (2 * frame + kind) + b
                rows_scr[k : k + 1, :] = value[:, b * 128 : (b + 1) * 128]

    def exchange_one(use):
        return [send(src1.at[use], buf1.at[use, j], peer) for j, peer in enumerate(peers1)]

    def exchange_two(use, copies):
        for copy in copies:
            copy.wait_recv()
        row8 = lax.broadcasted_iota(jnp.int32, (8, 128), 0)
        rows = jnp.zeros((8, 128), F32)
        for dx in range(NX):
            total = src1[use] if dx == 0 else buf1[use, NZ * dx - 1]
            for dz in range(1, NZ):
                total = total + buf1[use, NZ * dx + dz - 1]
            rows = rows + jnp.where(row8 == dx, total, 0.0)
        src2[use] = rows
        return [send(src2.at[use], buf2.at[use, j], peer) for j, peer in enumerate(peers2)]

    def params(use, copies, gain):
        for copy in copies:
            copy.wait_recv()
        lanes = lane_ids((8, 128))
        total = src2[use]
        for j in range(len(peers2)):
            total = total + buf2[use, j]
        parts = [jnp.broadcast_to(total[dx : dx + 1], (8, 128)) for dx in range(NX)]
        row8 = lax.broadcasted_iota(jnp.int32, (8, 128), 0)
        early = (lanes & 8) == 0
        for q in range(4):
            mixed = jnp.zeros((8, 128), F32)
            count = jnp.float32(0.0)
            for dx in range(NX):
                rr = lax.rem(r + NX - dx, NX)
                m0 = same(clip(2 * rr), clip_q[q])
                m1 = same(clip(2 * rr + 1), clip_q[q])
                count = count + m0 + m1
                mixed = mixed + jnp.where(early, m0, m1) * parts[dx]
            mixed = mixed + swap_lanes(mixed, 8)
            e_scr[8 * q : 8 * q + 8] = jnp.where((lanes & 15) == row8, mixed, 0.0)
            p_scr[8 * q : 8 * q + 8] = jnp.full((8, 128), jnp.maximum(count, 1.0), F32)
        e_scr[...] = segment_sum(e_scr[...]) / (p_scr[...] * float(128 * 80 * 512 // GROUPS))
        for q in range(4):
            mean = e_scr[8 * q : 8 * q + 4]
            scale = lax.rsqrt(e_scr[8 * q + 4 : 8 * q + 8] - mean * mean + 1e-06) * gain[...]
            p_scr[4 * q : 4 * q + 4] = scale
        for q in range(4):
            for b in range(4):
                mean_scr[q : q + 1, b * 128 : (b + 1) * 128] = e_scr[8 * q + b : 8 * q + b + 1, :]
                scale_scr[q : q + 1, b * 128 : (b + 1) * 128] = p_scr[4 * q + b : 4 * q + b + 1, :]

    def activated(value, q):
        v = (value - mean_scr[q : q + 1, :]) * scale_scr[q : q + 1, :]
        half = 0.5 * v
        return half + half * jnp.tanh(half)

    def place(value, q, row):
        if q == 3:
            act[2, 1, row] = value.astype(BF16)
        elif q == 2:
            act[2, 0, row] = value.astype(BF16)
            act[1, 1, row] = (value * pair[1, 1]).astype(BF16)
        elif q == 1:
            act[1, 0, row] = (value * pair[1, 0]).astype(BF16)
            act[0, 1, row] = (value * pair[0, 1]).astype(BF16)
        else:
            act[0, 0, row] = (value * pair[0, 0]).astype(BF16)

    def inside(row):
        out_top = one(row == 0) * one(t == 0)
        out_bottom = one(row == 5) * one(t == NT - 1)
        return (1 - out_top - out_bottom).astype(F32)

    def activate_rows(raw, q):
        @pl.loop(0, 6)
        def _(row):
            place(activated(raw[q, row].astype(F32), q) * inside(row), q, row)

    def activate_wide(q):
        @pl.loop(0, 4)
        def _(row):
            place(activated(mid[q - 2, row], q), q, row + 1)

        for row in (0, 5):
            place(activated(m_raw[q, row].astype(F32), q) * inside(row), q, row)

    def conv_step(w, frame, dx):
        lhs = jnp.concatenate(
            [act[dt, frame, dy : dy + 4].reshape(cells, 512) for dt in range(3) for dy in range(3)],
            axis=-1,
        )
        for n in range(2):
            cols = slice(n * 256, (n + 1) * 256)
            rhs = jnp.concatenate(
                [w[dt, dy, dx, :, cols] for dt in range(3) for dy in range(3)], axis=0
            )
            acc[dx, :, cols] = jnp.dot(lhs, rhs, preferred_element_type=F32)

    def conv(w, frame, start, stop):
        @pl.loop(start, stop)
        def _(dx):
            conv_step(w, frame, dx)

    def conv_row(row):
        rows = pl.ds(pl.multiple_of(row * width, 16), width)
        column = lax.broadcasted_iota(jnp.int32, (width, 512), 0)
        low = jnp.where(column == 0, 0.0, pltpu.roll(acc[0, rows, :], 1, 0))
        high = jnp.where(column == width - 1, 0.0, pltpu.roll(acc[2, rows, :], width - 1, 0))
        return acc[1, rows, :] + low + high

    def sums_of(value):
        parts = value.reshape(width // 8, 8, 512)
        return jnp.sum(parts, axis=0), jnp.sum(parts * parts, axis=0)

    zero = jnp.zeros((8, 512), F32)

    lat_copy.wait()
    for frame in range(2):
        def latent_row(row, carry, frame=frame):
            total, squares = sums_of(x_raw[2 + frame, row + 1].astype(F32))
            return carry[0] + total, carry[1] + squares

        put_rows(frame, *lax.fori_loop(0, 4, latent_row, (zero, zero)))
    pack(0)
    pl.semaphore_wait(barrier, len(greeted))

    def send_edges(src_rows, dst, frame):
        return [send(src_rows(frame, row, 1), dst.at[frame, row + 1 : row + 2], right) for row in (0, 3)]

    def send_inner(src_rows, dst, frame):
        return send(src_rows(frame, 1, 2), dst.at[frame, 2:4], right)

    def pass_edges(dst, q, edges):
        for edge in edges:
            edge.wait_recv()
        return [
            send(dst.at[q, 1:2], dst.at[q, 5:6], above),
            send(dst.at[q, 4:5], dst.at[q, 0:1], below),
        ]

    stats = exchange_one(0)

    def lat_rows(frame, row, n):
        return lat.at[frame, row : row + n]

    edges1 = send_edges(lat_rows, x_raw, 1)
    inner1 = send_inner(lat_rows, x_raw, 1)
    faces = [
        send(lat.at[0:2, 0:1], x_raw.at[2:4, 5:6], above),
        send(lat.at[0:2, 3:4], x_raw.at[2:4, 0:1], below),
    ]
    edges0 = send_edges(lat_rows, x_raw, 0)
    inner0 = send_inner(lat_rows, x_raw, 0)
    stats = exchange_two(0, stats)
    passed1 = pass_edges(x_raw, 1, edges1)
    params(0, stats, gain1)
    for copy in faces:
        copy.wait_recv()
    activate_rows(x_raw, 3)
    activate_rows(x_raw, 2)
    inner1.wait_recv()
    for copy in passed1:
        copy.wait_recv()
    activate_rows(x_raw, 1)
    w_copies[0].wait()
    conv(w1, 1, 0, 2)
    passed0 = pass_edges(x_raw, 0, edges0)
    conv(w1, 1, 2, 3)

    def finish_mid(frame):
        def mid_row(row, carry):
            value = conv_row(row)
            mid[frame, row] = value
            m_raw[2 + frame, row + 1] = value.astype(BF16)
            total, squares = sums_of(value)
            return carry[0] + total, carry[1] + squares

        put_rows(frame, *lax.fori_loop(0, 4, mid_row, (zero, zero)))

    def mid_rows(frame, row, n):
        return m_raw.at[2 + frame, row + 1 : row + 1 + n]

    def mid_faces(frame):
        return [
            send(m_raw.at[2 + frame, 1:2], m_raw.at[2 + frame, 5:6], above),
            send(m_raw.at[2 + frame, 4:5], m_raw.at[2 + frame, 0:1], below),
        ]

    finish_mid(1)
    edges1 = send_edges(mid_rows, m_raw, 1)
    faces = mid_faces(1)
    inner0.wait_recv()
    for copy in passed0:
        copy.wait_recv()
    activate_rows(x_raw, 0)
    conv(w1, 0, 0, 3)
    finish_mid(0)
    pack(1)
    stats = exchange_one(1)
    faces += mid_faces(0)
    inner1b = send_inner(mid_rows, m_raw, 1)
    edges0 = send_edges(mid_rows, m_raw, 0)
    inner0b = send_inner(mid_rows, m_raw, 0)
    stats = exchange_two(1, stats)
    passed1 = pass_edges(m_raw, 1, edges1)
    params(1, stats, gain2)
    for copy in faces:
        copy.wait_recv()
    activate_wide(3)
    activate_wide(2)
    inner1b.wait_recv()
    for copy in passed1:
        copy.wait_recv()
    activate_rows(m_raw, 1)
    w_copies[1].wait()
    passed0 = pass_edges(m_raw, 0, edges0)
    conv(w2, 1, 0, 3)

    def finish_out(frame):
        @pl.loop(0, 4)
        def _(row):
            stage[frame, row] = (x_raw[2 + frame, row + 1].astype(F32) + conv_row(row)).astype(BF16)

        copy = pltpu.make_async_copy(stage.at[frame], out.at[frame], local_sem.at[3 + frame])
        copy.start()
        return copy

    out1 = finish_out(1)
    inner0b.wait_recv()
    for copy in passed0:
        copy.wait_recv()
    activate_rows(m_raw, 0)
    conv(w2, 0, 0, 3)
    out0 = finish_out(0)
    for copy in sent:
        copy.wait_send()
    out1.wait()
    out0.wait()


N_SENDS = 2 * (NY * NC - 1) + 2 * (NX * NZ - 1) + 12 + 6 + 8


def shards(latents, lengths, conv_first, conv_second, gain_first, gain_second):
    frames, rows, width, chans = latents.shape
    smem = pl.BlockSpec(memory_space=pltpu.SMEM)
    vmem = pl.BlockSpec(memory_space=pltpu.VMEM)
    hbm = pl.BlockSpec(memory_space=pl.ANY)
    flops = 2 * 2 * frames * rows * width * 27 * chans * chans
    return pl.pallas_call(
        block_kernel,
        out_shape=jax.ShapeDtypeStruct(latents.shape, latents.dtype),
        in_specs=[smem, hbm, hbm, hbm, vmem, vmem],
        out_specs=hbm,
        scratch_shapes=[
            pltpu.VMEM(conv_first.shape, BF16),
            pltpu.VMEM(conv_second.shape, BF16),
            pltpu.VMEM((4, rows + 2, width, chans), BF16),
            pltpu.VMEM((4, rows + 2, width, chans), BF16),
            pltpu.VMEM((3, 2, rows + 2, width, chans), BF16),
            pltpu.VMEM((3, rows * width, chans), F32),
            pltpu.VMEM((2, rows, width, chans), F32),
            pltpu.VMEM((2, rows, width, chans), BF16),
            pltpu.VMEM((16, 128), F32),
            pltpu.VMEM((32, 128), F32),
            pltpu.VMEM((32, 128), F32),
            pltpu.VMEM((8, chans), F32),
            pltpu.VMEM((8, chans), F32),
            pltpu.VMEM((2, 8, 128), F32),
            pltpu.VMEM((2, NX * NZ - 1, 8, 128), F32),
            pltpu.VMEM((2, 8, 128), F32),
            pltpu.VMEM((2, NY * NC - 1, 8, 128), F32),
            pltpu.SemaphoreType.DMA((N_SENDS,)),
            pltpu.SemaphoreType.DMA((N_SENDS,)),
            pltpu.SemaphoreType.DMA((5,)),
        ],
        compiler_params=pltpu.CompilerParams(
            collective_id=0, has_side_effects=True, vmem_limit_bytes=60 * 2**20
        ),
        cost_estimate=pl.CostEstimate(
            flops=flops, bytes_accessed=2 * conv_first.size * 2 + 2 * latents.size * 2, transcendentals=latents.size * 6
        ),
    )(
        lengths, latents, conv_first, conv_second,
        gain_first.reshape(4, chans // 4), gain_second.reshape(4, chans // 4),
    )


def solution(mesh):
    return jax.shard_map(
        shards,
        mesh=mesh,
        in_specs=(P("req", "tile", None, None), P(), P(), P(), P(), P()),
        out_specs=P("req", "tile", None, None),
        check_vma=False,
    )
```

```python
import functools

import jax
import jax.numpy as jnp
from jax import lax
from jax.experimental import pallas as pl
from jax.experimental.pallas import tpu as pltpu
from jax.sharding import PartitionSpec as P

GROUPS = 32
MESH = pl.DeviceIdType.MESH
F32 = jnp.float32
BF16 = jnp.bfloat16
NX, NY, NZ, NC = 4, 4, 4, 2
NT = NZ * NY * NC


def lane_ids(shape):
    return lax.broadcasted_iota(jnp.int32, shape, 1)


def swap_lanes(x, step):
    lanes = lane_ids(x.shape)
    return jnp.where((lanes & step) != 0, pltpu.roll(x, step, 1), pltpu.roll(x, 128 - step, 1))


def segment_sum(x):
    for step in (1, 2, 4, 8):
        x = x + swap_lanes(x, step)
    return x


def block_kernel(
    lengths, lat, w1_hbm, w2_hbm, gain1, gain2, out,
    w1, w2, x_raw, m_raw, act, acc, mid, rows_scr, e_scr, p_scr, mean_scr, scale_scr,
    buf1, buf2, send_sem, recv_sem, local_sem,
):
    r = lax.axis_index("req")
    t = lax.axis_index("tile")
    cells = lat.shape[1] * lat.shape[2]
    width = lat.shape[2]
    here = NY * NC
    yc = lax.rem(t, here)
    plane = t - yc
    xs = [r] + [lax.rem(r + j, NX) for j in range(1, NX)]
    zs = [t] + [lax.rem(t + here * j, NT) for j in range(1, NZ)]
    right = (xs[1], t)
    above = (r, lax.rem(t + NT - 1, NT))
    below = (r, lax.rem(t + 1, NT))
    peers1 = [(xs[j // NZ], zs[j % NZ]) for j in range(1, NX * NZ)]
    peers2 = [(r, plane + lax.rem(yc + j, here)) for j in range(1, here)]

    def hops1(j):
        return min(j // NZ, NX - j // NZ) + min(j % NZ, NZ - j % NZ)

    def hops2(j):
        return min(j // NC, NY - j // NC)

    far1 = sorted(range(1, NX * NZ), key=hops1, reverse=True)
    far2 = sorted(range(1, here), key=hops2, reverse=True)
    barrier = pltpu.get_barrier_semaphore()
    greeted = [(hops1(j), peers1[j - 1]) for j in far1] + [(hops2(j), peers2[j - 1]) for j in far2]
    greeted += [(2, above), (2, below)]
    for _, peer in sorted(greeted, key=lambda entry: entry[0], reverse=True):
        pl.semaphore_signal(barrier, inc=1, device_id=peer, device_id_type=MESH)

    lat_copy = pltpu.make_async_copy(lat, x_raw.at[2:4, 1:5], local_sem.at[0])
    lat_copy.start()
    w_copies = [
        pltpu.make_async_copy(w1_hbm, w1, local_sem.at[1]),
        pltpu.make_async_copy(w2_hbm, w2, local_sem.at[2]),
    ]
    for copy in w_copies:
        copy.start()

    used = [0]
    sent = []

    def send(src, dst, peer):
        i = used[0]
        used[0] += 1
        copy = pltpu.make_async_remote_copy(
            src_ref=src, dst_ref=dst, send_sem=send_sem.at[i], recv_sem=recv_sem.at[i],
            device_id=peer, device_id_type=MESH,
        )
        copy.start()
        sent.append(copy)
        return copy

    first = lengths[0]
    second = first + lengths[1]
    third = second + lengths[2]

    def one(condition):
        return jnp.where(condition, 1, 0)

    def clip(s):
        return one(s >= 0) + one(s >= first) + one(s >= second) + one(s >= third) - 1

    base = 2 * r
    clip_q = [clip(base - 2 + q) for q in range(4)]

    def same(a, b):
        return jnp.where(a == b, 1.0, 0.0).astype(F32)

    pair = {
        (0, 0): same(clip_q[0], clip_q[2]),
        (1, 0): same(clip_q[1], clip_q[2]),
        (0, 1): same(clip_q[1], clip_q[3]),
        (1, 1): same(clip_q[2], clip_q[3]),
    }

    def pack(use):
        sums = segment_sum(rows_scr[...])
        row = lax.broadcasted_iota(jnp.int32, (16, 128), 0)
        picked = jnp.where((lane_ids((16, 128)) & 15) == row, sums, 0.0)
        buf1[use, 0:1] = jnp.sum(picked, axis=0, keepdims=True)

    def put_rows(frame, total, squares):
        for kind, value in enumerate((total, squares)):
            value = jnp.sum(value, axis=0, keepdims=True)
            for b in range(4):
                k = 4 * (2 * frame + kind) + b
                rows_scr[k : k + 1, :] = value[:, b * 128 : (b + 1) * 128]

    def exchange_one(use):
        return [send(buf1.at[use, 0:1], buf1.at[use, j : j + 1], peers1[j - 1]) for j in far1]

    def exchange_two(use, copies):
        for copy in copies:
            copy.wait_recv()
        for dx in range(NX):
            rows = [buf1[use, j : j + 1] for j in range(NZ * dx, NZ * dx + NZ)]
            buf2[use, 0, dx : dx + 1] = (rows[0] + rows[1]) + (rows[2] + rows[3])
        return [send(buf2.at[use, 0], buf2.at[use, j], peers2[j - 1]) for j in far2]

    def params(use, copies, gain):
        for copy in copies:
            copy.wait_recv()
        lanes = lane_ids((8, 128))
        total = buf2[use, 0]
        for j in range(1, here):
            total = total + buf2[use, j]
        parts = [jnp.broadcast_to(total[dx : dx + 1], (8, 128)) for dx in range(NX)]
        row8 = lax.broadcasted_iota(jnp.int32, (8, 128), 0)
        early = (lanes & 8) == 0
        for q in range(4):
            mixed = jnp.zeros((8, 128), F32)
            count = jnp.float32(0.0)
            for dx in range(NX):
                rr = lax.rem(r + NX - dx, NX)
                m0 = same(clip(2 * rr), clip_q[q])
                m1 = same(clip(2 * rr + 1), clip_q[q])
                count = count + m0 + m1
                mixed = mixed + jnp.where(early, m0, m1) * parts[dx]
            mixed = mixed + swap_lanes(mixed, 8)
            e_scr[8 * q : 8 * q + 8] = jnp.where((lanes & 15) == row8, mixed, 0.0)
            p_scr[8 * q : 8 * q + 8] = jnp.full((8, 128), jnp.maximum(count, 1.0), F32)
        e_scr[...] = segment_sum(e_scr[...]) / (p_scr[...] * float(128 * 80 * 512 // GROUPS))
        for q in range(4):
            mean = e_scr[8 * q : 8 * q + 4]
            scale = lax.rsqrt(e_scr[8 * q + 4 : 8 * q + 8] - mean * mean + 1e-06) * gain[...]
            p_scr[4 * q : 4 * q + 4] = scale
        for q in range(4):
            for b in range(4):
                mean_scr[q : q + 1, b * 128 : (b + 1) * 128] = e_scr[8 * q + b : 8 * q + b + 1, :]
                scale_scr[q : q + 1, b * 128 : (b + 1) * 128] = p_scr[4 * q + b : 4 * q + b + 1, :]

    def activated(value, q):
        v = (value - mean_scr[q : q + 1, :]) * scale_scr[q : q + 1, :]
        half = 0.5 * v
        return half + half * jnp.tanh(half)

    def place(value, q, row):
        if q == 3:
            act[2, 1, row] = value.astype(BF16)
        elif q == 2:
            act[2, 0, row] = value.astype(BF16)
            act[1, 1, row] = (value * pair[1, 1]).astype(BF16)
        elif q == 1:
            act[1, 0, row] = (value * pair[1, 0]).astype(BF16)
            act[0, 1, row] = (value * pair[0, 1]).astype(BF16)
        else:
            act[0, 0, row] = (value * pair[0, 0]).astype(BF16)

    def inside(row):
        out_top = one(row == 0) * one(t == 0)
        out_bottom = one(row == 5) * one(t == NT - 1)
        return (1 - out_top - out_bottom).astype(F32)

    def activate_rows(raw, q):
        @pl.loop(0, 6)
        def _(row):
            place(activated(raw[q, row].astype(F32), q) * inside(row), q, row)

    def activate_wide(q):
        @pl.loop(0, 4)
        def _(row):
            place(activated(mid[q - 2, row], q), q, row + 1)

        for row in (0, 5):
            place(activated(m_raw[q, row].astype(F32), q) * inside(row), q, row)

    def conv_step(w, frame, dx):
        lhs = jnp.concatenate(
            [act[dt, frame, dy : dy + 4].reshape(cells, 512) for dt in range(3) for dy in range(3)],
            axis=-1,
        )
        for n in range(2):
            cols = slice(n * 256, (n + 1) * 256)
            rhs = jnp.concatenate(
                [w[dt, dy, dx, :, cols] for dt in range(3) for dy in range(3)], axis=0
            )
            acc[dx, :, cols] = jnp.dot(lhs, rhs, preferred_element_type=F32)

    def conv(w, frame, start, stop):
        @pl.loop(start, stop)
        def _(dx):
            conv_step(w, frame, dx)

    def conv_row(row):
        rows = pl.ds(pl.multiple_of(row * width, 16), width)
        column = lax.broadcasted_iota(jnp.int32, (width, 512), 0)
        low = jnp.where(column == 0, 0.0, pltpu.roll(acc[0, rows, :], 1, 0))
        high = jnp.where(column == width - 1, 0.0, pltpu.roll(acc[2, rows, :], width - 1, 0))
        return acc[1, rows, :] + low + high

    def sums_of(value):
        parts = value.reshape(width // 8, 8, 512)
        return jnp.sum(parts, axis=0), jnp.sum(parts * parts, axis=0)

    zero = jnp.zeros((8, 512), F32)

    lat_copy.wait()
    for frame in range(2):
        def latent_row(row, carry, frame=frame):
            total, squares = sums_of(x_raw[2 + frame, row + 1].astype(F32))
            return carry[0] + total, carry[1] + squares

        put_rows(frame, *lax.fori_loop(0, 4, latent_row, (zero, zero)))
    pack(0)
    pl.semaphore_wait(barrier, len(greeted))

    def send_edges(src_rows, dst, frame):
        return [send(src_rows(frame, row, 1), dst.at[frame, row + 1 : row + 2], right) for row in (0, 3)]

    def send_inner(src_rows, dst, frame):
        return send(src_rows(frame, 1, 2), dst.at[frame, 2:4], right)

    def pass_edges(dst, q, edges):
        for edge in edges:
            edge.wait_recv()
        return [
            send(dst.at[q, 1:2], dst.at[q, 5:6], above),
            send(dst.at[q, 4:5], dst.at[q, 0:1], below),
        ]

    stats = exchange_one(0)

    def lat_rows(frame, row, n):
        return lat.at[frame, row : row + n]

    edges1 = send_edges(lat_rows, x_raw, 1)
    inner1 = send_inner(lat_rows, x_raw, 1)
    faces = [
        send(lat.at[0:2, 0:1], x_raw.at[2:4, 5:6], above),
        send(lat.at[0:2, 3:4], x_raw.at[2:4, 0:1], below),
    ]
    stats = exchange_two(0, stats)
    edges0 = send_edges(lat_rows, x_raw, 0)
    inner0 = send_inner(lat_rows, x_raw, 0)
    passed1 = pass_edges(x_raw, 1, edges1)
    params(0, stats, gain1)
    for copy in faces:
        copy.wait_recv()
    activate_rows(x_raw, 3)
    activate_rows(x_raw, 2)
    inner1.wait_recv()
    for copy in passed1:
        copy.wait_recv()
    activate_rows(x_raw, 1)
    w_copies[0].wait()
    conv(w1, 1, 0, 1)
    passed0 = pass_edges(x_raw, 0, edges0)
    conv(w1, 1, 1, 3)

    def finish_mid(frame):
        def mid_row(row, carry):
            value = conv_row(row)
            mid[frame, row] = value
            m_raw[2 + frame, row + 1] = value.astype(BF16)
            total, squares = sums_of(value)
            return carry[0] + total, carry[1] + squares

        put_rows(frame, *lax.fori_loop(0, 4, mid_row, (zero, zero)))

    def mid_rows(frame, row, n):
        return m_raw.at[2 + frame, row + 1 : row + 1 + n]

    def mid_faces(frame):
        return [
            send(m_raw.at[2 + frame, 1:2], m_raw.at[2 + frame, 5:6], above),
            send(m_raw.at[2 + frame, 4:5], m_raw.at[2 + frame, 0:1], below),
        ]

    finish_mid(1)
    edges1 = send_edges(mid_rows, m_raw, 1)
    faces = mid_faces(1)
    inner0.wait_recv()
    for copy in passed0:
        copy.wait_recv()
    activate_rows(x_raw, 0)
    conv(w1, 0, 0, 3)
    finish_mid(0)
    pack(1)
    stats = exchange_one(1)
    faces += mid_faces(0)
    inner1b = send_inner(mid_rows, m_raw, 1)
    stats = exchange_two(1, stats)
    edges0 = send_edges(mid_rows, m_raw, 0)
    inner0b = send_inner(mid_rows, m_raw, 0)
    passed1 = pass_edges(m_raw, 1, edges1)
    params(1, stats, gain2)
    for copy in faces:
        copy.wait_recv()
    activate_wide(3)
    activate_wide(2)
    inner1b.wait_recv()
    for copy in passed1:
        copy.wait_recv()
    activate_rows(m_raw, 1)
    w_copies[1].wait()
    passed0 = pass_edges(m_raw, 0, edges0)
    conv(w2, 1, 0, 3)

    def finish_out(frame):
        @pl.loop(0, 4)
        def _(row):
            out[frame, row] = (x_raw[2 + frame, row + 1].astype(F32) + conv_row(row)).astype(BF16)


    finish_out(1)
    inner0b.wait_recv()
    for copy in passed0:
        copy.wait_recv()
    activate_rows(m_raw, 0)
    conv(w2, 0, 0, 3)
    finish_out(0)
    for copy in sent:
        copy.wait_send()


N_SENDS = 2 * (NY * NC - 1) + 2 * (NX * NZ - 1) + 12 + 6 + 8


def shards(latents, lengths, conv_first, conv_second, gain_first, gain_second):
    frames, rows, width, chans = latents.shape
    smem = pl.BlockSpec(memory_space=pltpu.SMEM)
    vmem = pl.BlockSpec(memory_space=pltpu.VMEM)
    hbm = pl.BlockSpec(memory_space=pl.ANY)
    flops = 2 * 2 * frames * rows * width * 27 * chans * chans
    return pl.pallas_call(
        block_kernel,
        out_shape=pltpu.VMEM(latents.shape, latents.dtype),
        in_specs=[smem, hbm, hbm, hbm, vmem, vmem],
        out_specs=pl.BlockSpec(memory_space=pltpu.VMEM),
        scratch_shapes=[
            pltpu.VMEM(conv_first.shape, BF16),
            pltpu.VMEM(conv_second.shape, BF16),
            pltpu.VMEM((4, rows + 2, width, chans), BF16),
            pltpu.VMEM((4, rows + 2, width, chans), BF16),
            pltpu.VMEM((3, 2, rows + 2, width, chans), BF16),
            pltpu.VMEM((3, rows * width, chans), F32),
            pltpu.VMEM((2, rows, width, chans), F32),
            pltpu.VMEM((16, 128), F32),
            pltpu.VMEM((32, 128), F32),
            pltpu.VMEM((32, 128), F32),
            pltpu.VMEM((8, chans), F32),
            pltpu.VMEM((8, chans), F32),
            pltpu.VMEM((2, NX * NZ, 128), F32),
            pltpu.VMEM((2, NY * NC, NX, 128), F32),
            pltpu.SemaphoreType.DMA((N_SENDS,)),
            pltpu.SemaphoreType.DMA((N_SENDS,)),
            pltpu.SemaphoreType.DMA((3,)),
        ],
        compiler_params=pltpu.CompilerParams(
            collective_id=0, has_side_effects=True, vmem_limit_bytes=60 * 2**20
        ),
        cost_estimate=pl.CostEstimate(
            flops=flops, bytes_accessed=2 * conv_first.size * 2 + 2 * latents.size * 2, transcendentals=latents.size * 6
        ),
    )(
        lengths, latents, conv_first, conv_second,
        gain_first.reshape(4, chans // 4), gain_second.reshape(4, chans // 4),
    )


def solution(mesh):
    return jax.shard_map(
        shards,
        mesh=mesh,
        in_specs=(P("req", "tile", None, None), P(), P(), P(), P(), P()),
        out_specs=P("req", "tile", None, None),
        check_vma=False,
    )
```

```python
import functools

import jax
import jax.numpy as jnp
from jax import lax
from jax.experimental import pallas as pl
from jax.experimental.pallas import tpu as pltpu
from jax.sharding import PartitionSpec as P

GROUPS = 32
MESH = pl.DeviceIdType.MESH
F32 = jnp.float32
BF16 = jnp.bfloat16
NX, NY, NZ, NC = 4, 4, 4, 2
NT = NZ * NY * NC


def lane_ids(shape):
    return lax.broadcasted_iota(jnp.int32, shape, 1)


def swap_lanes(x, step):
    lanes = lane_ids(x.shape)
    return jnp.where((lanes & step) != 0, pltpu.roll(x, step, 1), pltpu.roll(x, 128 - step, 1))


def segment_sum(x):
    for step in (1, 2, 4, 8):
        x = x + swap_lanes(x, step)
    return x


def block_kernel(
    lengths, lat, w1_hbm, w2_hbm, gain1, gain2, out,
    w1, w2, x_raw, m_raw, act, acc, mid, rows_scr, e_scr, p_scr, mean_scr, scale_scr,
    buf0, buf1, send_sem, recv_sem, chip_sem, local_sem,
):
    r = lax.axis_index("req")
    t = lax.axis_index("tile")
    cells = lat.shape[1] * lat.shape[2]
    width = lat.shape[2]
    here = NY * NC
    yc = lax.rem(t, here)
    core = lax.rem(t, NC)
    plane = t - yc
    xs = [r] + [lax.rem(r + j, NX) for j in range(1, NX)]
    planes = [plane] + [lax.rem(plane + here * j, NT) for j in range(1, NZ)]
    ys = [yc] + [lax.rem(yc + NC * j, here) for j in range(1, NY)]
    right = (xs[1], t)
    sibling = (r, t + 1 - 2 * core)
    above = (r, lax.rem(t + NT - 1, NT))
    below = (r, lax.rem(t + 1, NT))
    chips = NX * NY * NZ

    def steps(j):
        return j // (NY * NZ), (j // NZ) % NY, j % NZ

    def hops(j):
        dx, dy, dz = steps(j)
        return min(dx, NX - dx) + min(dy, NY - dy) + min(dz, NZ - dz)

    def peer(j):
        dx, dy, dz = steps(j)
        return (xs[dx], planes[dz] + ys[dy])

    far = sorted(range(1, chips), key=hops, reverse=True)
    barrier = pltpu.get_barrier_semaphore()
    greeted = [peer(j) for j in far] + [above, below, sibling]
    for other in greeted:
        pl.semaphore_signal(barrier, inc=1, device_id=other, device_id_type=MESH)

    lat_copy = pltpu.make_async_copy(lat, x_raw.at[2:4, 1:5], local_sem.at[0])
    lat_copy.start()
    w_copies = [
        pltpu.make_async_copy(w1_hbm, w1, local_sem.at[1]),
        pltpu.make_async_copy(w2_hbm, w2, local_sem.at[2]),
    ]
    for copy in w_copies:
        copy.start()

    used = [0]
    sent = []

    def send(src, dst, peer):
        i = used[0]
        used[0] += 1
        copy = pltpu.make_async_remote_copy(
            src_ref=src, dst_ref=dst, send_sem=send_sem.at[i], recv_sem=recv_sem.at[i],
            device_id=peer, device_id_type=MESH,
        )
        copy.start()
        sent.append(copy)
        return copy

    first = lengths[0]
    second = first + lengths[1]
    third = second + lengths[2]

    def one(condition):
        return jnp.where(condition, 1, 0)

    def clip(s):
        return one(s >= 0) + one(s >= first) + one(s >= second) + one(s >= third) - 1

    base = 2 * r
    clip_q = [clip(base - 2 + q) for q in range(4)]

    def same(a, b):
        return jnp.where(a == b, 1.0, 0.0).astype(F32)

    pair = {
        (0, 0): same(clip_q[0], clip_q[2]),
        (1, 0): same(clip_q[1], clip_q[2]),
        (0, 1): same(clip_q[1], clip_q[3]),
        (1, 1): same(clip_q[2], clip_q[3]),
    }

    def pack(use):
        sums = segment_sum(rows_scr[...])
        row = lax.broadcasted_iota(jnp.int32, (16, 128), 0)
        picked = jnp.where((lane_ids((16, 128)) & 15) == row, sums, 0.0)
        buf0[use, 0:1] = jnp.sum(picked, axis=0, keepdims=True)

    def put_rows(frame, total, squares):
        for kind, value in enumerate((total, squares)):
            value = jnp.sum(value, axis=0, keepdims=True)
            for b in range(4):
                k = 4 * (2 * frame + kind) + b
                rows_scr[k : k + 1, :] = value[:, b * 128 : (b + 1) * 128]

    def exchange_one(use):
        return send(buf0.at[use, 0:1], buf0.at[use, 1:2], sibling)

    def rows_of_others(use):
        return buf1.at[use, 1:chips]

    def exchange_two(use, copy):
        copy.wait_recv()
        buf1[use, 0:1] = buf0[use, 0:1] + buf0[use, 1:2]
        for j in far:
            pltpu.make_async_remote_copy(
                src_ref=buf1.at[use, 0:1], dst_ref=buf1.at[use, j : j + 1], send_sem=chip_sem.at[use],
                recv_sem=chip_sem.at[2 + use], device_id=peer(j), device_id_type=MESH,
            ).start()

    def chips_done(use, sem):
        pltpu.make_async_copy(rows_of_others(use), rows_of_others(use), chip_sem.at[sem]).wait()

    def params(use, gain):
        chips_done(use, 2 + use)
        lanes = lane_ids((8, 128))
        per_x = NY * NZ
        parts = []
        for dx in range(NX):
            total = jnp.sum(buf1[use, dx * per_x : (dx + 1) * per_x], axis=0, keepdims=True)
            parts.append(jnp.broadcast_to(total, (8, 128)))
        row8 = lax.broadcasted_iota(jnp.int32, (8, 128), 0)
        early = (lanes & 8) == 0
        for q in range(4):
            mixed = jnp.zeros((8, 128), F32)
            count = jnp.float32(0.0)
            for dx in range(NX):
                rr = lax.rem(r + NX - dx, NX)
                m0 = same(clip(2 * rr), clip_q[q])
                m1 = same(clip(2 * rr + 1), clip_q[q])
                count = count + m0 + m1
                mixed = mixed + jnp.where(early, m0, m1) * parts[dx]
            mixed = mixed + swap_lanes(mixed, 8)
            e_scr[8 * q : 8 * q + 8] = jnp.where((lanes & 15) == row8, mixed, 0.0)
            p_scr[8 * q : 8 * q + 8] = jnp.full((8, 128), jnp.maximum(count, 1.0), F32)
        e_scr[...] = segment_sum(e_scr[...]) / (p_scr[...] * float(128 * 80 * 512 // GROUPS))
        for q in range(4):
            mean = e_scr[8 * q : 8 * q + 4]
            scale = lax.rsqrt(e_scr[8 * q + 4 : 8 * q + 8] - mean * mean + 1e-06) * gain[...]
            p_scr[4 * q : 4 * q + 4] = scale
        for q in range(4):
            for b in range(4):
                mean_scr[q : q + 1, b * 128 : (b + 1) * 128] = e_scr[8 * q + b : 8 * q + b + 1, :]
                scale_scr[q : q + 1, b * 128 : (b + 1) * 128] = p_scr[4 * q + b : 4 * q + b + 1, :]

    def activated(value, q):
        v = (value - mean_scr[q : q + 1, :]) * scale_scr[q : q + 1, :]
        half = 0.5 * v
        return half + half * jnp.tanh(half)

    def place(value, q, row):
        if q == 3:
            act[2, 1, row] = value.astype(BF16)
        elif q == 2:
            act[2, 0, row] = value.astype(BF16)
            act[1, 1, row] = (value * pair[1, 1]).astype(BF16)
        elif q == 1:
            act[1, 0, row] = (value * pair[1, 0]).astype(BF16)
            act[0, 1, row] = (value * pair[0, 1]).astype(BF16)
        else:
            act[0, 0, row] = (value * pair[0, 0]).astype(BF16)

    def inside(row):
        out_top = one(row == 0) * one(t == 0)
        out_bottom = one(row == 5) * one(t == NT - 1)
        return (1 - out_top - out_bottom).astype(F32)

    def activate_rows(raw, q):
        @pl.loop(0, 6)
        def _(row):
            place(activated(raw[q, row].astype(F32), q) * inside(row), q, row)

    def activate_wide(q):
        @pl.loop(0, 4)
        def _(row):
            place(activated(mid[q - 2, row], q), q, row + 1)

        for row in (0, 5):
            place(activated(m_raw[q, row].astype(F32), q) * inside(row), q, row)

    def conv_step(w, frame, dx):
        lhs = jnp.concatenate(
            [act[dt, frame, dy : dy + 4].reshape(cells, 512) for dt in range(3) for dy in range(3)],
            axis=-1,
        )
        for n in range(2):
            cols = slice(n * 256, (n + 1) * 256)
            rhs = jnp.concatenate(
                [w[dt, dy, dx, :, cols] for dt in range(3) for dy in range(3)], axis=0
            )
            acc[dx, :, cols] = jnp.dot(lhs, rhs, preferred_element_type=F32)

    def conv(w, frame, start, stop):
        @pl.loop(start, stop)
        def _(dx):
            conv_step(w, frame, dx)

    def conv_row(row):
        rows = pl.ds(pl.multiple_of(row * width, 16), width)
        column = lax.broadcasted_iota(jnp.int32, (width, 512), 0)
        low = jnp.where(column == 0, 0.0, pltpu.roll(acc[0, rows, :], 1, 0))
        high = jnp.where(column == width - 1, 0.0, pltpu.roll(acc[2, rows, :], width - 1, 0))
        return acc[1, rows, :] + low + high

    def sums_of(value):
        parts = value.reshape(width // 8, 8, 512)
        return jnp.sum(parts, axis=0), jnp.sum(parts * parts, axis=0)

    zero = jnp.zeros((8, 512), F32)

    lat_copy.wait()
    for frame in range(2):
        def latent_row(row, carry, frame=frame):
            total, squares = sums_of(x_raw[2 + frame, row + 1].astype(F32))
            return carry[0] + total, carry[1] + squares

        put_rows(frame, *lax.fori_loop(0, 4, latent_row, (zero, zero)))
    pack(0)
    pl.semaphore_wait(barrier, len(greeted))

    def send_edges(src_rows, dst, frame):
        return [send(src_rows(frame, row, 1), dst.at[frame, row + 1 : row + 2], right) for row in (0, 3)]

    def send_inner(src_rows, dst, frame):
        return send(src_rows(frame, 1, 2), dst.at[frame, 2:4], right)

    def pass_edges(dst, q, edges):
        for edge in edges:
            edge.wait_recv()
        return [
            send(dst.at[q, 1:2], dst.at[q, 5:6], above),
            send(dst.at[q, 4:5], dst.at[q, 0:1], below),
        ]

    stats = exchange_one(0)

    def lat_rows(frame, row, n):
        return x_raw.at[2 + frame, row + 1 : row + 1 + n]

    edges1 = send_edges(lat_rows, x_raw, 1)
    exchange_two(0, stats)
    faces = [
        send(lat.at[0:2, 0:1], x_raw.at[2:4, 5:6], above),
        send(lat.at[0:2, 3:4], x_raw.at[2:4, 0:1], below),
    ]
    inner1 = send_inner(lat_rows, x_raw, 1)
    edges0 = send_edges(lat_rows, x_raw, 0)
    inner0 = send_inner(lat_rows, x_raw, 0)
    passed1 = pass_edges(x_raw, 1, edges1)
    params(0, gain1)
    for copy in faces:
        copy.wait_recv()
    activate_rows(x_raw, 3)
    activate_rows(x_raw, 2)
    inner1.wait_recv()
    for copy in passed1:
        copy.wait_recv()
    activate_rows(x_raw, 1)
    w_copies[0].wait()
    conv(w1, 1, 0, 1)
    passed0 = pass_edges(x_raw, 0, edges0)
    conv(w1, 1, 1, 3)

    def finish_mid(frame):
        def mid_row(row, carry):
            value = conv_row(row)
            mid[frame, row] = value
            m_raw[2 + frame, row + 1] = value.astype(BF16)
            total, squares = sums_of(value)
            return carry[0] + total, carry[1] + squares

        put_rows(frame, *lax.fori_loop(0, 4, mid_row, (zero, zero)))

    def mid_rows(frame, row, n):
        return m_raw.at[2 + frame, row + 1 : row + 1 + n]

    def mid_faces(frame):
        return [
            send(m_raw.at[2 + frame, 1:2], m_raw.at[2 + frame, 5:6], above),
            send(m_raw.at[2 + frame, 4:5], m_raw.at[2 + frame, 0:1], below),
        ]

    finish_mid(1)
    edges1 = send_edges(mid_rows, m_raw, 1)
    inner1b = send_inner(mid_rows, m_raw, 1)
    faces = mid_faces(1)
    inner0.wait_recv()
    for copy in passed0:
        copy.wait_recv()
    activate_rows(x_raw, 0)
    conv(w1, 0, 0, 3)
    finish_mid(0)
    pack(1)
    stats = exchange_one(1)
    exchange_two(1, stats)
    faces += mid_faces(0)
    edges0 = send_edges(mid_rows, m_raw, 0)
    inner0b = send_inner(mid_rows, m_raw, 0)
    passed1 = pass_edges(m_raw, 1, edges1)
    params(1, gain2)
    for copy in faces:
        copy.wait_recv()
    activate_wide(3)
    activate_wide(2)
    inner1b.wait_recv()
    for copy in passed1:
        copy.wait_recv()
    activate_rows(m_raw, 1)
    w_copies[1].wait()
    passed0 = pass_edges(m_raw, 0, edges0)
    conv(w2, 1, 0, 3)

    def finish_out(frame):
        @pl.loop(0, 4)
        def _(row):
            out[frame, row] = (x_raw[2 + frame, row + 1].astype(F32) + conv_row(row)).astype(BF16)


    finish_out(1)
    inner0b.wait_recv()
    for copy in passed0:
        copy.wait_recv()
    activate_rows(m_raw, 0)
    conv(w2, 0, 0, 3)
    finish_out(0)
    for copy in sent:
        copy.wait_send()
    for use in range(2):
        chips_done(use, use)


N_SENDS = 2 + 12 + 6 + 8


def shards(latents, lengths, conv_first, conv_second, gain_first, gain_second):
    frames, rows, width, chans = latents.shape
    smem = pl.BlockSpec(memory_space=pltpu.SMEM)
    vmem = pl.BlockSpec(memory_space=pltpu.VMEM)
    hbm = pl.BlockSpec(memory_space=pl.ANY)
    flops = 2 * 2 * frames * rows * width * 27 * chans * chans
    return pl.pallas_call(
        block_kernel,
        out_shape=pltpu.VMEM(latents.shape, latents.dtype),
        in_specs=[smem, hbm, hbm, hbm, vmem, vmem],
        out_specs=pl.BlockSpec(memory_space=pltpu.VMEM),
        scratch_shapes=[
            pltpu.VMEM(conv_first.shape, BF16),
            pltpu.VMEM(conv_second.shape, BF16),
            pltpu.VMEM((4, rows + 2, width, chans), BF16),
            pltpu.VMEM((4, rows + 2, width, chans), BF16),
            pltpu.VMEM((3, 2, rows + 2, width, chans), BF16),
            pltpu.VMEM((3, rows * width, chans), F32),
            pltpu.VMEM((2, rows, width, chans), F32),
            pltpu.VMEM((16, 128), F32),
            pltpu.VMEM((32, 128), F32),
            pltpu.VMEM((32, 128), F32),
            pltpu.VMEM((8, chans), F32),
            pltpu.VMEM((8, chans), F32),
            pltpu.VMEM((2, 8, 128), F32),
            pltpu.VMEM((2, NX * NY * NZ, 128), F32),
            pltpu.SemaphoreType.DMA((N_SENDS,)),
            pltpu.SemaphoreType.DMA((N_SENDS,)),
            pltpu.SemaphoreType.DMA((4,)),
            pltpu.SemaphoreType.DMA((3,)),
        ],
        compiler_params=pltpu.CompilerParams(
            collective_id=0, has_side_effects=True, vmem_limit_bytes=60 * 2**20
        ),
        cost_estimate=pl.CostEstimate(
            flops=flops, bytes_accessed=2 * conv_first.size * 2 + 2 * latents.size * 2, transcendentals=latents.size * 6
        ),
    )(
        lengths, latents, conv_first, conv_second,
        gain_first.reshape(4, chans // 4), gain_second.reshape(4, chans // 4),
    )


def solution(mesh):
    return jax.shard_map(
        shards,
        mesh=mesh,
        in_specs=(P("req", "tile", None, None), P(), P(), P(), P(), P()),
        out_specs=P("req", "tile", None, None),
        check_vma=False,
    )
```

```python
import functools

import jax
import jax.numpy as jnp
from jax import lax
from jax.experimental import pallas as pl
from jax.experimental.pallas import tpu as pltpu
from jax.sharding import PartitionSpec as P

GROUPS = 32
MESH = pl.DeviceIdType.MESH
F32 = jnp.float32
BF16 = jnp.bfloat16
NX, NY, NZ, NC = 4, 4, 4, 2
NT = NZ * NY * NC


def lane_ids(shape):
    return lax.broadcasted_iota(jnp.int32, shape, 1)


def swap_lanes(x, step):
    lanes = lane_ids(x.shape)
    return jnp.where((lanes & step) != 0, pltpu.roll(x, step, 1), pltpu.roll(x, 128 - step, 1))


def segment_sum(x):
    for step in (1, 2, 4, 8):
        x = x + swap_lanes(x, step)
    return x


def block_kernel(
    lengths, lat, w1_hbm, w2_hbm, gain1, gain2, out,
    w1, w2, x_raw, m_raw, act, acc, mid, rows_scr, e_scr, p_scr, mean_scr, scale_scr,
    buf0, buf1, send_sem, recv_sem, chip_sem, local_sem,
):
    r = lax.axis_index("req")
    t = lax.axis_index("tile")
    cells = lat.shape[1] * lat.shape[2]
    width = lat.shape[2]
    here = NY * NC
    yc = lax.rem(t, here)
    core = lax.rem(t, NC)
    plane = t - yc
    xs = [r] + [lax.rem(r + j, NX) for j in range(1, NX)]
    planes = [plane] + [lax.rem(plane + here * j, NT) for j in range(1, NZ)]
    ys = [yc] + [lax.rem(yc + NC * j, here) for j in range(1, NY)]
    right = (xs[1], t)
    sibling = (r, t + 1 - 2 * core)
    above = (r, lax.rem(t + NT - 1, NT))
    below = (r, lax.rem(t + 1, NT))
    chips = NX * NY * NZ

    def steps(j):
        return j // (NY * NZ), (j // NZ) % NY, j % NZ

    def hops(j):
        dx, dy, dz = steps(j)
        return min(dx, NX - dx) + min(dy, NY - dy) + min(dz, NZ - dz)

    def peer(j):
        dx, dy, dz = steps(j)
        return (xs[dx], planes[dz] + ys[dy])

    far = sorted(range(1, chips), key=hops, reverse=True)
    barrier = pltpu.get_barrier_semaphore()
    greeted = [peer(j) for j in far] + [above, below, sibling]
    for other in greeted:
        pl.semaphore_signal(barrier, inc=1, device_id=other, device_id_type=MESH)

    lat_copy = pltpu.make_async_copy(lat, x_raw.at[2:4, 1:5], local_sem.at[0])
    lat_copy.start()
    w_copies = [
        pltpu.make_async_copy(w1_hbm, w1, local_sem.at[1]),
        pltpu.make_async_copy(w2_hbm, w2, local_sem.at[2]),
    ]
    for copy in w_copies:
        copy.start()

    used = [0]
    sent = []

    def send(src, dst, peer):
        i = used[0]
        used[0] += 1
        copy = pltpu.make_async_remote_copy(
            src_ref=src, dst_ref=dst, send_sem=send_sem.at[i], recv_sem=recv_sem.at[i],
            device_id=peer, device_id_type=MESH,
        )
        copy.start()
        sent.append(copy)
        return copy

    first = lengths[0]
    second = first + lengths[1]
    third = second + lengths[2]

    def one(condition):
        return jnp.where(condition, 1, 0)

    def clip(s):
        return one(s >= 0) + one(s >= first) + one(s >= second) + one(s >= third) - 1

    base = 2 * r
    clip_q = [clip(base - 2 + q) for q in range(4)]

    def same(a, b):
        return jnp.where(a == b, 1.0, 0.0).astype(F32)

    pair = {
        (0, 0): same(clip_q[0], clip_q[2]),
        (1, 0): same(clip_q[1], clip_q[2]),
        (0, 1): same(clip_q[1], clip_q[3]),
        (1, 1): same(clip_q[2], clip_q[3]),
    }

    def pack(use):
        sums = segment_sum(rows_scr[...])
        row = lax.broadcasted_iota(jnp.int32, (16, 128), 0)
        picked = jnp.where((lane_ids((16, 128)) & 15) == row, sums, 0.0)
        buf0[use, 0:1] = jnp.sum(picked, axis=0, keepdims=True)

    def put_rows(frame, total, squares):
        for kind, value in enumerate((total, squares)):
            value = jnp.sum(value, axis=0, keepdims=True)
            for b in range(4):
                k = 4 * (2 * frame + kind) + b
                rows_scr[k : k + 1, :] = value[:, b * 128 : (b + 1) * 128]

    def exchange_one(use):
        return send(buf0.at[use, 0:1], buf0.at[use, 1:2], sibling)

    def rows_of_others(use):
        return buf1.at[use, 1:chips]

    def exchange_two(use, copy):
        copy.wait_recv()
        buf1[use, 0:1] = buf0[use, 0:1] + buf0[use, 1:2]
        for j in far:
            pltpu.make_async_remote_copy(
                src_ref=buf1.at[use, 0:1], dst_ref=buf1.at[use, j : j + 1], send_sem=chip_sem.at[use],
                recv_sem=chip_sem.at[2 + use], device_id=peer(j), device_id_type=MESH,
            ).start()

    def chips_done(use, sem):
        pltpu.make_async_copy(rows_of_others(use), rows_of_others(use), chip_sem.at[sem]).wait()

    def params(use, gain):
        chips_done(use, 2 + use)
        lanes = lane_ids((8, 128))
        per_x = NY * NZ
        parts = []
        for dx in range(NX):
            total = jnp.sum(buf1[use, dx * per_x : (dx + 1) * per_x], axis=0, keepdims=True)
            parts.append(jnp.broadcast_to(total, (8, 128)))
        row8 = lax.broadcasted_iota(jnp.int32, (8, 128), 0)
        early = (lanes & 8) == 0
        for q in range(4):
            mixed = jnp.zeros((8, 128), F32)
            count = jnp.float32(0.0)
            for dx in range(NX):
                rr = lax.rem(r + NX - dx, NX)
                m0 = same(clip(2 * rr), clip_q[q])
                m1 = same(clip(2 * rr + 1), clip_q[q])
                count = count + m0 + m1
                mixed = mixed + jnp.where(early, m0, m1) * parts[dx]
            mixed = mixed + swap_lanes(mixed, 8)
            e_scr[8 * q : 8 * q + 8] = jnp.where((lanes & 15) == row8, mixed, 0.0)
            p_scr[8 * q : 8 * q + 8] = jnp.full((8, 128), jnp.maximum(count, 1.0), F32)
        e_scr[...] = segment_sum(e_scr[...]) / (p_scr[...] * float(128 * 80 * 512 // GROUPS))
        for q in range(4):
            mean = e_scr[8 * q : 8 * q + 4]
            scale = lax.rsqrt(e_scr[8 * q + 4 : 8 * q + 8] - mean * mean + 1e-06) * gain[...]
            p_scr[4 * q : 4 * q + 4] = scale
        for q in range(4):
            for b in range(4):
                mean_scr[q : q + 1, b * 128 : (b + 1) * 128] = e_scr[8 * q + b : 8 * q + b + 1, :]
                scale_scr[q : q + 1, b * 128 : (b + 1) * 128] = p_scr[4 * q + b : 4 * q + b + 1, :]

    def activated(value, q):
        v = (value - mean_scr[q : q + 1, :]) * scale_scr[q : q + 1, :]
        half = 0.5 * v
        return half + half * jnp.tanh(half)

    def place(value, q, row):
        if q == 3:
            act[2, 1, row] = value.astype(BF16)
        elif q == 2:
            act[2, 0, row] = value.astype(BF16)
            act[1, 1, row] = (value * pair[1, 1]).astype(BF16)
        elif q == 1:
            act[1, 0, row] = (value * pair[1, 0]).astype(BF16)
            act[0, 1, row] = (value * pair[0, 1]).astype(BF16)
        else:
            act[0, 0, row] = (value * pair[0, 0]).astype(BF16)

    def inside(row):
        out_top = one(row == 0) * one(t == 0)
        out_bottom = one(row == 5) * one(t == NT - 1)
        return (1 - out_top - out_bottom).astype(F32)

    def activate_rows(raw, q):
        @pl.loop(0, 6)
        def _(row):
            place(activated(raw[q, row].astype(F32), q) * inside(row), q, row)

    def activate_wide(q):
        @pl.loop(0, 4)
        def _(row):
            place(activated(mid[q - 2, row], q), q, row + 1)

        for row in (0, 5):
            place(activated(m_raw[q, row].astype(F32), q) * inside(row), q, row)

    def conv_step(w, frame, dx):
        lhs = jnp.concatenate(
            [act[dt, frame, dy : dy + 4].reshape(cells, 512) for dt in range(3) for dy in range(3)],
            axis=-1,
        )
        for n in range(2):
            cols = slice(n * 256, (n + 1) * 256)
            rhs = jnp.concatenate(
                [w[dt, dy, dx, :, cols] for dt in range(3) for dy in range(3)], axis=0
            )
            acc[dx, :, cols] = jnp.dot(lhs, rhs, preferred_element_type=F32)

    def conv(w, frame, start, stop):
        @pl.loop(start, stop)
        def _(dx):
            conv_step(w, frame, dx)

    def conv_row(row):
        rows = pl.ds(pl.multiple_of(row * width, 16), width)
        column = lax.broadcasted_iota(jnp.int32, (width, 512), 0)
        low = jnp.where(column == 0, 0.0, pltpu.roll(acc[0, rows, :], 1, 0))
        high = jnp.where(column == width - 1, 0.0, pltpu.roll(acc[2, rows, :], width - 1, 0))
        return acc[1, rows, :] + low + high

    def sums_of(value):
        parts = value.reshape(width // 8, 8, 512)
        return jnp.sum(parts, axis=0), jnp.sum(parts * parts, axis=0)

    zero = jnp.zeros((8, 512), F32)

    lat_copy.wait()
    for frame in range(2):
        def latent_row(row, carry, frame=frame):
            total, squares = sums_of(x_raw[2 + frame, row + 1].astype(F32))
            return carry[0] + total, carry[1] + squares

        put_rows(frame, *lax.fori_loop(0, 4, latent_row, (zero, zero)))
    pack(0)
    pl.semaphore_wait(barrier, len(greeted))

    def send_edges(src_rows, dst, frame):
        return [send(src_rows(frame, row, 1), dst.at[frame, row + 1 : row + 2], right) for row in (0, 3)]

    def send_inner(src_rows, dst, frame):
        return send(src_rows(frame, 1, 2), dst.at[frame, 2:4], right)

    def pass_edges(dst, q, edges):
        edges[0].wait_recv()
        up = send(dst.at[q, 1:2], dst.at[q, 5:6], above)
        edges[1].wait_recv()
        return [up, send(dst.at[q, 4:5], dst.at[q, 0:1], below)]

    stats = exchange_one(0)

    def lat_rows(frame, row, n):
        return x_raw.at[2 + frame, row + 1 : row + 1 + n]

    edges1 = send_edges(lat_rows, x_raw, 1)
    exchange_two(0, stats)
    faces = [
        send(lat.at[0:2, 0:1], x_raw.at[2:4, 5:6], above),
        send(lat.at[0:2, 3:4], x_raw.at[2:4, 0:1], below),
    ]
    inner1 = send_inner(lat_rows, x_raw, 1)
    edges0 = send_edges(lat_rows, x_raw, 0)
    inner0 = send_inner(lat_rows, x_raw, 0)
    passed1 = pass_edges(x_raw, 1, edges1)
    params(0, gain1)
    for copy in faces:
        copy.wait_recv()
    activate_rows(x_raw, 3)
    activate_rows(x_raw, 2)
    inner1.wait_recv()
    for copy in passed1:
        copy.wait_recv()
    activate_rows(x_raw, 1)
    w_copies[0].wait()
    conv(w1, 1, 0, 1)
    passed0 = pass_edges(x_raw, 0, edges0)
    conv(w1, 1, 1, 3)

    def finish_mid(frame):
        def mid_row(row, carry):
            value = conv_row(row)
            mid[frame, row] = value
            m_raw[2 + frame, row + 1] = value.astype(BF16)
            total, squares = sums_of(value)
            return carry[0] + total, carry[1] + squares

        put_rows(frame, *lax.fori_loop(0, 4, mid_row, (zero, zero)))

    def mid_rows(frame, row, n):
        return m_raw.at[2 + frame, row + 1 : row + 1 + n]

    def mid_faces(frame):
        return [
            send(m_raw.at[2 + frame, 1:2], m_raw.at[2 + frame, 5:6], above),
            send(m_raw.at[2 + frame, 4:5], m_raw.at[2 + frame, 0:1], below),
        ]

    finish_mid(1)
    edges1 = send_edges(mid_rows, m_raw, 1)
    inner1b = send_inner(mid_rows, m_raw, 1)
    faces = mid_faces(1)
    inner0.wait_recv()
    for copy in passed0:
        copy.wait_recv()
    activate_rows(x_raw, 0)
    conv(w1, 0, 0, 3)
    finish_mid(0)
    pack(1)
    stats = exchange_one(1)
    exchange_two(1, stats)
    faces += mid_faces(0)
    edges0 = send_edges(mid_rows, m_raw, 0)
    inner0b = send_inner(mid_rows, m_raw, 0)
    passed1 = pass_edges(m_raw, 1, edges1)
    params(1, gain2)
    for copy in faces:
        copy.wait_recv()
    activate_wide(3)
    activate_wide(2)
    inner1b.wait_recv()
    for copy in passed1:
        copy.wait_recv()
    activate_rows(m_raw, 1)
    w_copies[1].wait()
    passed0 = pass_edges(m_raw, 0, edges0)
    conv(w2, 1, 0, 3)

    def finish_out(frame):
        @pl.loop(0, 4)
        def _(row):
            out[frame, row] = (x_raw[2 + frame, row + 1].astype(F32) + conv_row(row)).astype(BF16)


    finish_out(1)
    inner0b.wait_recv()
    for copy in passed0:
        copy.wait_recv()
    activate_rows(m_raw, 0)
    conv(w2, 0, 0, 3)
    finish_out(0)
    for copy in sent:
        copy.wait_send()
    for use in range(2):
        chips_done(use, use)


N_SENDS = 2 + 12 + 6 + 8


def shards(latents, lengths, conv_first, conv_second, gain_first, gain_second):
    frames, rows, width, chans = latents.shape
    smem = pl.BlockSpec(memory_space=pltpu.SMEM)
    vmem = pl.BlockSpec(memory_space=pltpu.VMEM)
    hbm = pl.BlockSpec(memory_space=pl.ANY)
    flops = 2 * 2 * frames * rows * width * 27 * chans * chans
    return pl.pallas_call(
        block_kernel,
        out_shape=pltpu.VMEM(latents.shape, latents.dtype),
        in_specs=[smem, hbm, hbm, hbm, vmem, vmem],
        out_specs=pl.BlockSpec(memory_space=pltpu.VMEM),
        scratch_shapes=[
            pltpu.VMEM(conv_first.shape, BF16),
            pltpu.VMEM(conv_second.shape, BF16),
            pltpu.VMEM((4, rows + 2, width, chans), BF16),
            pltpu.VMEM((4, rows + 2, width, chans), BF16),
            pltpu.VMEM((3, 2, rows + 2, width, chans), BF16),
            pltpu.VMEM((3, rows * width, chans), F32),
            pltpu.VMEM((2, rows, width, chans), F32),
            pltpu.VMEM((16, 128), F32),
            pltpu.VMEM((32, 128), F32),
            pltpu.VMEM((32, 128), F32),
            pltpu.VMEM((8, chans), F32),
            pltpu.VMEM((8, chans), F32),
            pltpu.VMEM((2, 8, 128), F32),
            pltpu.VMEM((2, NX * NY * NZ, 128), F32),
            pltpu.SemaphoreType.DMA((N_SENDS,)),
            pltpu.SemaphoreType.DMA((N_SENDS,)),
            pltpu.SemaphoreType.DMA((4,)),
            pltpu.SemaphoreType.DMA((3,)),
        ],
        compiler_params=pltpu.CompilerParams(
            collective_id=0, has_side_effects=True, vmem_limit_bytes=60 * 2**20
        ),
        cost_estimate=pl.CostEstimate(
            flops=flops, bytes_accessed=2 * conv_first.size * 2 + 2 * latents.size * 2, transcendentals=latents.size * 6
        ),
    )(
        lengths, latents, conv_first, conv_second,
        gain_first.reshape(4, chans // 4), gain_second.reshape(4, chans // 4),
    )


def solution(mesh):
    return jax.shard_map(
        shards,
        mesh=mesh,
        in_specs=(P("req", "tile", None, None), P(), P(), P(), P(), P()),
        out_specs=P("req", "tile", None, None),
        check_vma=False,
    )
```

```python
import functools

import jax
import jax.numpy as jnp
from jax import lax
from jax.experimental import pallas as pl
from jax.experimental.pallas import tpu as pltpu
from jax.sharding import PartitionSpec as P

GROUPS = 32
MESH = pl.DeviceIdType.MESH
F32 = jnp.float32
BF16 = jnp.bfloat16
NX, NY, NZ, NC = 4, 4, 4, 2
NT = NZ * NY * NC


def lane_ids(shape):
    return lax.broadcasted_iota(jnp.int32, shape, 1)


def swap_lanes(x, step):
    lanes = lane_ids(x.shape)
    return jnp.where((lanes & step) != 0, pltpu.roll(x, step, 1), pltpu.roll(x, 128 - step, 1))


def segment_sum(x):
    for step in (1, 2, 4, 8):
        x = x + swap_lanes(x, step)
    return x


def block_kernel(
    lengths, lat, w1_hbm, w2_hbm, gain1, gain2, out,
    w1, w2, x_raw, m_raw, act, acc, mid, rows_scr, e_scr, p_scr, mean_scr, scale_scr,
    buf0, buf1, send_sem, recv_sem, chip_sem, local_sem,
):
    r = lax.axis_index("req")
    t = lax.axis_index("tile")
    cells = lat.shape[1] * lat.shape[2]
    width = lat.shape[2]
    here = NY * NC
    yc = lax.rem(t, here)
    core = lax.rem(t, NC)
    plane = t - yc
    xs = [r] + [lax.rem(r + j, NX) for j in range(1, NX)]
    planes = [plane] + [lax.rem(plane + here * j, NT) for j in range(1, NZ)]
    ys = [yc] + [lax.rem(yc + NC * j, here) for j in range(1, NY)]
    right = (xs[1], t)
    sibling = (r, t + 1 - 2 * core)
    above = (r, lax.rem(t + NT - 1, NT))
    below = (r, lax.rem(t + 1, NT))
    chips = NX * NY * NZ

    def steps(j):
        return j // (NY * NZ), (j // NZ) % NY, j % NZ

    def hops(j):
        dx, dy, dz = steps(j)
        return min(dx, NX - dx) + min(dy, NY - dy) + min(dz, NZ - dz)

    def peer(j):
        dx, dy, dz = steps(j)
        return (xs[dx], planes[dz] + ys[dy])

    far = sorted(range(1, chips), key=hops, reverse=True)
    barrier = pltpu.get_barrier_semaphore()
    greeted = [peer(j) for j in far] + [above, below, sibling]
    for other in greeted:
        pl.semaphore_signal(barrier, inc=1, device_id=other, device_id_type=MESH)

    lat_copy = pltpu.make_async_copy(lat, x_raw.at[2:4, 1:5], local_sem.at[0])
    lat_copy.start()
    w_copies = [
        pltpu.make_async_copy(w1_hbm, w1, local_sem.at[1]),
        pltpu.make_async_copy(w2_hbm, w2, local_sem.at[2]),
    ]
    for copy in w_copies:
        copy.start()

    used = [0]
    sent = []

    def send(src, dst, peer):
        i = used[0]
        used[0] += 1
        copy = pltpu.make_async_remote_copy(
            src_ref=src, dst_ref=dst, send_sem=send_sem.at[i], recv_sem=recv_sem.at[i],
            device_id=peer, device_id_type=MESH,
        )
        copy.start()
        sent.append(copy)
        return copy

    first = lengths[0]
    second = first + lengths[1]
    third = second + lengths[2]

    def one(condition):
        return jnp.where(condition, 1, 0)

    def clip(s):
        return one(s >= 0) + one(s >= first) + one(s >= second) + one(s >= third) - 1

    base = 2 * r
    clip_q = [clip(base - 2 + q) for q in range(4)]

    def same(a, b):
        return jnp.where(a == b, 1.0, 0.0).astype(F32)

    pair = {
        (0, 0): same(clip_q[0], clip_q[2]),
        (1, 0): same(clip_q[1], clip_q[2]),
        (0, 1): same(clip_q[1], clip_q[3]),
        (1, 1): same(clip_q[2], clip_q[3]),
    }

    def pack(use):
        sums = segment_sum(rows_scr[...])
        row = lax.broadcasted_iota(jnp.int32, (16, 128), 0)
        picked = jnp.where((lane_ids((16, 128)) & 15) == row, sums, 0.0)
        buf0[use, 0:1] = jnp.sum(picked, axis=0, keepdims=True)

    def put_rows(frame, total, squares):
        for kind, value in enumerate((total, squares)):
            value = jnp.sum(value, axis=0, keepdims=True)
            for b in range(4):
                k = 4 * (2 * frame + kind) + b
                rows_scr[k : k + 1, :] = value[:, b * 128 : (b + 1) * 128]

    def exchange_one(use):
        return send(buf0.at[use, 0:1], buf0.at[use, 1:2], sibling)

    def rows_of_others(use):
        return buf1.at[use, 1:chips]

    def exchange_two(use, copy):
        copy.wait_recv()
        buf1[use, 0:1] = buf0[use, 0:1] + buf0[use, 1:2]
        for j in far:
            pltpu.make_async_remote_copy(
                src_ref=buf1.at[use, 0:1], dst_ref=buf1.at[use, j : j + 1], send_sem=chip_sem.at[use],
                recv_sem=chip_sem.at[2 + use], device_id=peer(j), device_id_type=MESH,
            ).start()

    def chips_done(use, sem):
        pltpu.make_async_copy(rows_of_others(use), rows_of_others(use), chip_sem.at[sem]).wait()

    def params(use, gain):
        chips_done(use, 2 + use)
        lanes = lane_ids((8, 128))
        per_x = NY * NZ
        parts = []
        for dx in range(NX):
            total = jnp.sum(buf1[use, dx * per_x : (dx + 1) * per_x], axis=0, keepdims=True)
            parts.append(jnp.broadcast_to(total, (8, 128)))
        row8 = lax.broadcasted_iota(jnp.int32, (8, 128), 0)
        early = (lanes & 8) == 0
        for q in range(4):
            mixed = jnp.zeros((8, 128), F32)
            count = jnp.float32(0.0)
            for dx in range(NX):
                rr = lax.rem(r + NX - dx, NX)
                m0 = same(clip(2 * rr), clip_q[q])
                m1 = same(clip(2 * rr + 1), clip_q[q])
                count = count + m0 + m1
                mixed = mixed + jnp.where(early, m0, m1) * parts[dx]
            mixed = mixed + swap_lanes(mixed, 8)
            e_scr[8 * q : 8 * q + 8] = jnp.where((lanes & 15) == row8, mixed, 0.0)
            p_scr[8 * q : 8 * q + 8] = jnp.full((8, 128), jnp.maximum(count, 1.0), F32)
        e_scr[...] = segment_sum(e_scr[...]) / (p_scr[...] * float(128 * 80 * 512 // GROUPS))
        for q in range(4):
            mean = e_scr[8 * q : 8 * q + 4]
            scale = lax.rsqrt(e_scr[8 * q + 4 : 8 * q + 8] - mean * mean + 1e-06) * gain[...]
            p_scr[4 * q : 4 * q + 4] = scale
        for q in range(4):
            for b in range(4):
                mean_scr[q : q + 1, b * 128 : (b + 1) * 128] = e_scr[8 * q + b : 8 * q + b + 1, :]
                scale_scr[q : q + 1, b * 128 : (b + 1) * 128] = p_scr[4 * q + b : 4 * q + b + 1, :]

    def activated(value, q):
        v = (value - mean_scr[q : q + 1, :]) * scale_scr[q : q + 1, :]
        half = 0.5 * v
        return half + half * jnp.tanh(half)

    def place(value, q, row):
        if q == 3:
            act[2, 1, row] = value.astype(BF16)
        elif q == 2:
            act[2, 0, row] = value.astype(BF16)
            act[1, 1, row] = (value * pair[1, 1]).astype(BF16)
        elif q == 1:
            act[1, 0, row] = (value * pair[1, 0]).astype(BF16)
            act[0, 1, row] = (value * pair[0, 1]).astype(BF16)
        else:
            act[0, 0, row] = (value * pair[0, 0]).astype(BF16)

    def inside(row):
        out_top = one(row == 0) * one(t == 0)
        out_bottom = one(row == 5) * one(t == NT - 1)
        return (1 - out_top - out_bottom).astype(F32)

    def activate_rows(raw, q):
        @pl.loop(0, 6)
        def _(row):
            place(activated(raw[q, row].astype(F32), q) * inside(row), q, row)

    def activate_wide(q):
        @pl.loop(0, 4)
        def _(row):
            place(activated(mid[q - 2, row], q), q, row + 1)

        for row in (0, 5):
            place(activated(m_raw[q, row].astype(F32), q) * inside(row), q, row)

    def conv_step(w, frame, dx):
        lhs = jnp.concatenate(
            [act[dt, frame, dy : dy + 4].reshape(cells, 512) for dt in range(3) for dy in range(3)],
            axis=-1,
        )
        for n in range(2):
            cols = slice(n * 256, (n + 1) * 256)
            rhs = jnp.concatenate(
                [w[dt, dy, dx, :, cols] for dt in range(3) for dy in range(3)], axis=0
            )
            acc[dx, :, cols] = jnp.dot(lhs, rhs, preferred_element_type=F32)

    def conv(w, frame, start, stop):
        @pl.loop(start, stop)
        def _(dx):
            conv_step(w, frame, dx)

    def conv_row(row):
        rows = pl.ds(pl.multiple_of(row * width, 16), width)
        column = lax.broadcasted_iota(jnp.int32, (width, 512), 0)
        low = jnp.where(column == 0, 0.0, pltpu.roll(acc[0, rows, :], 1, 0))
        high = jnp.where(column == width - 1, 0.0, pltpu.roll(acc[2, rows, :], width - 1, 0))
        return acc[1, rows, :] + low + high

    def sums_of(value):
        parts = value.reshape(width // 8, 8, 512)
        return jnp.sum(parts, axis=0), jnp.sum(parts * parts, axis=0)

    zero = jnp.zeros((8, 512), F32)

    lat_copy.wait()
    for frame in range(2):
        def latent_row(row, carry, frame=frame):
            total, squares = sums_of(x_raw[2 + frame, row + 1].astype(F32))
            return carry[0] + total, carry[1] + squares

        put_rows(frame, *lax.fori_loop(0, 4, latent_row, (zero, zero)))
    pack(0)
    pl.semaphore_wait(barrier, len(greeted))

    def send_edges(src_rows, dst, frame):
        return [send(src_rows(frame, row, 1), dst.at[frame, row + 1 : row + 2], right) for row in (0, 3)]

    def send_inner(src_rows, dst, frame):
        return send(src_rows(frame, 1, 2), dst.at[frame, 2:4], right)

    def pass_edges(dst, q, edges):
        edges[0].wait_recv()
        up = send(dst.at[q, 1:2], dst.at[q, 5:6], above)
        edges[1].wait_recv()
        return [up, send(dst.at[q, 4:5], dst.at[q, 0:1], below)]

    stats = exchange_one(0)

    def lat_rows(frame, row, n):
        return x_raw.at[2 + frame, row + 1 : row + 1 + n]

    edges1 = send_edges(lat_rows, x_raw, 1)
    exchange_two(0, stats)
    faces = [
        send(lat.at[0:2, 0:1], x_raw.at[2:4, 5:6], above),
        send(lat.at[0:2, 3:4], x_raw.at[2:4, 0:1], below),
    ]
    edges0 = send_edges(lat_rows, x_raw, 0)
    inner1 = send_inner(lat_rows, x_raw, 1)
    inner0 = send_inner(lat_rows, x_raw, 0)
    passed1 = pass_edges(x_raw, 1, edges1)
    params(0, gain1)
    for copy in faces:
        copy.wait_recv()
    activate_rows(x_raw, 3)
    activate_rows(x_raw, 2)
    inner1.wait_recv()
    for copy in passed1:
        copy.wait_recv()
    activate_rows(x_raw, 1)
    w_copies[0].wait()
    conv(w1, 1, 0, 1)
    passed0 = pass_edges(x_raw, 0, edges0)
    conv(w1, 1, 1, 3)

    def finish_mid(frame):
        def mid_row(row, carry):
            value = conv_row(row)
            mid[frame, row] = value
            m_raw[2 + frame, row + 1] = value.astype(BF16)
            total, squares = sums_of(value)
            return carry[0] + total, carry[1] + squares

        put_rows(frame, *lax.fori_loop(0, 4, mid_row, (zero, zero)))

    def mid_rows(frame, row, n):
        return m_raw.at[2 + frame, row + 1 : row + 1 + n]

    def mid_faces(frame):
        return [
            send(m_raw.at[2 + frame, 1:2], m_raw.at[2 + frame, 5:6], above),
            send(m_raw.at[2 + frame, 4:5], m_raw.at[2 + frame, 0:1], below),
        ]

    finish_mid(1)
    edges1 = send_edges(mid_rows, m_raw, 1)
    inner1b = send_inner(mid_rows, m_raw, 1)
    faces = mid_faces(1)
    inner0.wait_recv()
    for copy in passed0:
        copy.wait_recv()
    activate_rows(x_raw, 0)
    conv(w1, 0, 0, 3)
    finish_mid(0)
    pack(1)
    stats = exchange_one(1)
    exchange_two(1, stats)
    faces += mid_faces(0)
    edges0 = send_edges(mid_rows, m_raw, 0)
    inner0b = send_inner(mid_rows, m_raw, 0)
    passed1 = pass_edges(m_raw, 1, edges1)
    params(1, gain2)
    for copy in faces:
        copy.wait_recv()
    activate_wide(3)
    activate_wide(2)
    inner1b.wait_recv()
    for copy in passed1:
        copy.wait_recv()
    activate_rows(m_raw, 1)
    w_copies[1].wait()
    passed0 = pass_edges(m_raw, 0, edges0)
    conv(w2, 1, 0, 3)

    def finish_out(frame):
        @pl.loop(0, 4)
        def _(row):
            out[frame, row] = (x_raw[2 + frame, row + 1].astype(F32) + conv_row(row)).astype(BF16)


    finish_out(1)
    inner0b.wait_recv()
    for copy in passed0:
        copy.wait_recv()
    activate_rows(m_raw, 0)
    conv(w2, 0, 0, 3)
    finish_out(0)
    for copy in sent:
        copy.wait_send()
    for use in range(2):
        chips_done(use, use)


N_SENDS = 2 + 12 + 6 + 8


def shards(latents, lengths, conv_first, conv_second, gain_first, gain_second):
    frames, rows, width, chans = latents.shape
    smem = pl.BlockSpec(memory_space=pltpu.SMEM)
    vmem = pl.BlockSpec(memory_space=pltpu.VMEM)
    hbm = pl.BlockSpec(memory_space=pl.ANY)
    flops = 2 * 2 * frames * rows * width * 27 * chans * chans
    return pl.pallas_call(
        block_kernel,
        out_shape=pltpu.VMEM(latents.shape, latents.dtype),
        in_specs=[smem, hbm, hbm, hbm, vmem, vmem],
        out_specs=pl.BlockSpec(memory_space=pltpu.VMEM),
        scratch_shapes=[
            pltpu.VMEM(conv_first.shape, BF16),
            pltpu.VMEM(conv_second.shape, BF16),
            pltpu.VMEM((4, rows + 2, width, chans), BF16),
            pltpu.VMEM((4, rows + 2, width, chans), BF16),
            pltpu.VMEM((3, 2, rows + 2, width, chans), BF16),
            pltpu.VMEM((3, rows * width, chans), F32),
            pltpu.VMEM((2, rows, width, chans), F32),
            pltpu.VMEM((16, 128), F32),
            pltpu.VMEM((32, 128), F32),
            pltpu.VMEM((32, 128), F32),
            pltpu.VMEM((8, chans), F32),
            pltpu.VMEM((8, chans), F32),
            pltpu.VMEM((2, 8, 128), F32),
            pltpu.VMEM((2, NX * NY * NZ, 128), F32),
            pltpu.SemaphoreType.DMA((N_SENDS,)),
            pltpu.SemaphoreType.DMA((N_SENDS,)),
            pltpu.SemaphoreType.DMA((4,)),
            pltpu.SemaphoreType.DMA((3,)),
        ],
        compiler_params=pltpu.CompilerParams(
            collective_id=0, has_side_effects=True, vmem_limit_bytes=60 * 2**20
        ),
        cost_estimate=pl.CostEstimate(
            flops=flops, bytes_accessed=2 * conv_first.size * 2 + 2 * latents.size * 2, transcendentals=latents.size * 6
        ),
    )(
        lengths, latents, conv_first, conv_second,
        gain_first.reshape(4, chans // 4), gain_second.reshape(4, chans // 4),
    )


def solution(mesh):
    return jax.shard_map(
        shards,
        mesh=mesh,
        in_specs=(P("req", "tile", None, None), P(), P(), P(), P(), P()),
        out_specs=P("req", "tile", None, None),
        check_vma=False,
    )
```
